32 devices in a mesh: dp: 16 (over z, y, x), fsdp: 2 (over core).
Axes of the slice: x: 2, y: 2, z: 4, core: 2. Of those that a mesh axis runs over, the one named last changes fastest.
Arguments:
- tokens: bfloat16 [4, 32, 128, 576], P(None, ('dp', 'fsdp')), may hold values from -6 to 6
- cotangent: bfloat16 [4, 32, 128, 576], P(None, ('dp', 'fsdp')), may hold values from -6 to 6
- lengths: int32 [4, 32, 4], P(None, ('dp', 'fsdp')), may hold values from 0 to 128, as said below
- w_query: bfloat16 [576, 576], P('fsdp'), may hold values from -0.25 to 0.25
- w_key: bfloat16 [576, 192], P('fsdp'), may hold values from -0.25 to 0.25
- w_value: bfloat16 [576, 192], P('fsdp'), may hold values from -0.25 to 0.25
- w_out: bfloat16 [576, 576], P('fsdp'), may hold values from -1 to 1
- w_gate: bfloat16 [576, 1536], P('fsdp'), may hold values from -0.25 to 0.25
- w_up: bfloat16 [576, 1536], P('fsdp'), may hold values from -0.25 to 0.25
- w_down: bfloat16 [1536, 576], P('fsdp'), may hold values from -0.15625 to 0.15625
- gain_attn: bfloat16 [576], P('fsdp'), may hold values from 0.5 to 1.5
- gain_ffn: bfloat16 [576], P('fsdp'), may hold values from 0.5 to 1.5
Outputs:
- output: bfloat16 [4, 32, 128, 576], P(None, ('dp', 'fsdp'))
- input_grad: float32 [4, 32, 128, 576], P(None, ('dp', 'fsdp'))
- grad_query: float32 [576, 576], P('fsdp')
- grad_key: float32 [576, 192], P('fsdp')
- grad_value: float32 [576, 192], P('fsdp')
- grad_out: float32 [576, 576], P('fsdp')
- grad_gate: float32 [576, 1536], P('fsdp')
- grad_up: float32 [576, 1536], P('fsdp')
- grad_down: float32 [1536, 576], P('fsdp')
- grad_gain_attn: float32 [576], P('fsdp')
- grad_gain_ffn: float32 [576], P('fsdp')
The draws below stay inside these ranges and needn't reach their ends.
Inputs may be any that keep to these rules, and one draw needn't show every extreme that they name: lengths[m, b] lists the sequences packed in order from the start of bucket b of micro-batch m; zeros are empty slots; a row sums to at most 128 and the rest of the bucket is padding. Row [0, 0] is one sequence that fills its bucket.
All inputs are finite; a program needn't handle non-finite values.
Results may differ from the reference program's by a relative error of at most 0.022.
Values may be sent and summed in bfloat16 or wider, within the bound.
A program may use at most 192 MiB of HBM per device.

```python
import math
import jax
import jax.numpy as jnp
from jax import lax

D = 576
HEADS = 9
KV_HEADS = 3
HD = 64
FF = 1536
BUCKET = 128
PACK = 4
MB = 4
QW = 576
KVW = 192
NB = 32


def draw_lengths(key, part):
    key = jax.random.fold_in(key, 17)
    key_powers, key_extra, key_padding = jax.random.split(key, 3)
    draw_shape = (MB, NB, PACK)
    powers = jax.random.randint(key_powers, draw_shape, 0, 5)
    unit_len = max(BUCKET // 16, 1)
    base_len = unit_len * jnp.left_shift(jnp.ones(draw_shape, jnp.int32), powers.astype(jnp.int32))
    extra_len = jax.random.randint(key_extra, draw_shape, 0, 1 << 30) % base_len
    raw_len = jnp.minimum(base_len + extra_len, BUCKET)
    padding = jax.random.randint(key_padding, (MB, NB, 1), 0, BUCKET // 4 + 1)
    bucket_limit = BUCKET - padding
    seq_ends = jnp.minimum(jnp.cumsum(raw_len, axis=-1).astype(jnp.int32), bucket_limit)
    seq_starts = jnp.concatenate([jnp.zeros((MB, NB, 1), jnp.int32), seq_ends[..., :-1]], axis=-1)
    drawn = (seq_ends - seq_starts).astype(jnp.int32)
    full_row = jnp.zeros((PACK,), jnp.int32).at[0].set(BUCKET)
    drawn = drawn.at[0, 0].set(full_row)
    return drawn.astype(jnp.int32)


def shard_levels(key, shape, shards, smallest, largest):
    loudness, own = 1.0, jax.random.fold_in(key, 6)
    for dim, parts in shards:
        draws = jnp.exp(jax.random.uniform(jax.random.fold_in(own, dim), (parts,), jnp.float32, smallest / len(shards), largest / len(shards)))
        loudness = loudness * jnp.repeat(draws, shape[dim] // parts).reshape([-1 if axis == dim else 1 for axis in range(len(shape))])
    return loudness


def scatter_about(stream_key, extent, deviation, most, shards=(), kind=jnp.bfloat16):
    values = deviation * jax.random.normal(stream_key, extent, jnp.float32)
    if shards:
        values = values * shard_levels(stream_key, extent, shards, -0.22, 0.18)
    return jnp.clip(values, -most, most).astype(kind)


def setup_inputs(seed: int = 0) -> dict:
    splits = jax.random.split(jax.random.key(seed), 13)
    tokens = scatter_about(splits[0], (MB, NB, BUCKET, D), 1.0, 6.0, ((1, 32),))
    cotangent = scatter_about(splits[1], (MB, NB, BUCKET, D), 1.0, 6.0, ((1, 32),))
    lengths = draw_lengths(jax.random.fold_in(splits[12], 71), 0)
    w_query = scatter_about(splits[3], (D, QW), D ** -0.5, 0.25, ((0, 2),))
    w_key = scatter_about(splits[4], (D, KVW), D ** -0.5, 0.25, ((0, 2),))
    w_value = scatter_about(splits[5], (D, KVW), D ** -0.5, 0.25, ((0, 2),))
    w_out = scatter_about(splits[6], (QW, D), (QW // 16) ** -0.5, 1.0, ((0, 2),))
    w_gate = scatter_about(splits[7], (D, FF), D ** -0.5, 0.25, ((0, 2),))
    w_up = scatter_about(splits[8], (D, FF), D ** -0.5, 0.25, ((0, 2),))
    w_down = scatter_about(splits[9], (FF, D), FF ** -0.5, 0.15625, ((0, 2),))
    gain_attn = jnp.clip(1.0 + 0.1 * jax.random.normal(splits[10], (D,), jnp.float32), 0.5, 1.5).astype(jnp.bfloat16)
    gain_ffn = jnp.clip(1.0 + 0.1 * jax.random.normal(splits[11], (D,), jnp.float32), 0.5, 1.5).astype(jnp.bfloat16)
    return dict(tokens=tokens, cotangent=cotangent, lengths=lengths, w_query=w_query, w_key=w_key, w_value=w_value, w_out=w_out, w_gate=w_gate, w_up=w_up, w_down=w_down, gain_attn=gain_attn, gain_ffn=gain_ffn)


@jax.custom_vjp
def low(v):
    return lax.optimization_barrier(v.astype(jnp.bfloat16)).astype(jnp.float32)

@jax.custom_vjp
def low_back(v):
    return v

def low_keep(v):
    return (low(v), None)

def low_pass(kept, grad):
    return (grad,)

def back_keep(v):
    return (v, None)

def back_low(kept, grad):
    return (low(grad),)
low.defvjp(low_keep, low_pass)
low_back.defvjp(back_keep, back_low)
HIGH = lax.Precision.HIGHEST

def segment_tables(lengths_row, count):
    bounds = jnp.cumsum(lengths_row).astype(jnp.int32)
    places = jnp.arange(count, dtype=jnp.int32)
    segment = lax.optimization_barrier(jnp.sum((places[:, None] >= bounds[None, :]).astype(jnp.int32), axis=1)).astype(jnp.int32)
    starts = jnp.concatenate([jnp.zeros((1,), jnp.int32), bounds])
    matches = segment[:, None] == jnp.arange(starts.shape[0], dtype=jnp.int32)[None, :]
    seg_begin = lax.optimization_barrier(jnp.sum(jnp.where(matches, starts[None, :], 0), axis=1)).astype(jnp.int32)
    offset = places - seg_begin
    live_mask = (places < bounds[-1]).astype(jnp.float32)
    allowed = (segment[:, None] == segment[None, :]) & (places[None, :] <= places[:, None])
    return (offset, live_mask, allowed)

def rope_tables(offset, head_dim):
    half_dim = head_dim // 2
    inverse = jnp.exp(jnp.arange(half_dim, dtype=jnp.float32) * (-2.0 * math.log(10000.0) / head_dim))
    angles = offset.astype(jnp.float32)[:, None] * inverse[None, :]
    return (jnp.cos(angles)[:, None, :], jnp.sin(angles)[:, None, :])

def rotate(values, cosines, sines):
    half_dim = values.shape[-1] // 2
    lower_half = values[..., :half_dim]
    upper_half = values[..., half_dim:]
    return jnp.concatenate([lower_half * cosines - upper_half * sines, upper_half * cosines + lower_half * sines], axis=-1)

def rms_norm(rows, gain):
    return rows * lax.rsqrt(lax.optimization_barrier(jnp.mean(rows * rows, axis=-1, keepdims=True)) + 1e-05) * gain

def product(left, right):
    return jnp.dot(left, right, precision=HIGH)

def attend(query, key, value, allowed):
    count, heads, head_dim = query.shape
    kv_heads = key.shape[1]
    group_size = heads // kv_heads
    grouped = query.reshape(count, kv_heads, group_size, head_dim)
    scores = jnp.einsum('qkgd,pkd->kgqp', grouped, key, precision=HIGH) * (1.0 / math.sqrt(head_dim))
    scores = low_back(scores)
    scores = jnp.where(allowed[None, None], scores, -1000000000.0)
    probs = low(jax.nn.softmax(scores, axis=-1))
    mixed = jnp.einsum('kgqp,pkd->qkgd', probs, value, precision=HIGH)
    return mixed.reshape(count, heads * head_dim)

def block_pass(rows, weights, tables):
    w_query, w_key, w_value, w_out, w_gate, w_up, w_down, gain_attn, gain_ffn = weights
    cosines, sines, allowed = tables
    count = rows.shape[0]
    normed_one = low(rms_norm(rows, gain_attn))
    query_raw = low_back(product(normed_one, w_query))
    key_raw = low_back(product(normed_one, w_key))
    value = low(low_back(product(normed_one, w_value))).reshape(count, KV_HEADS, HD)
    query = low(rotate(query_raw.reshape(count, HEADS, HD), cosines, sines))
    key = low(rotate(key_raw.reshape(count, KV_HEADS, HD), cosines, sines))
    attn_out = low(low_back(attend(query, key, value, allowed)))
    middle = rows + low_back(product(attn_out, w_out))
    normed_two = low(rms_norm(middle, gain_ffn))
    gate_out = low_back(product(normed_two, w_gate))
    up_out = low_back(product(normed_two, w_up))
    hidden = low(jax.nn.silu(gate_out) * up_out)
    return middle + low_back(product(hidden, w_down))

def reference(tokens, cotangent, lengths, w_query, w_key, w_value, w_out, w_gate, w_up, w_down, gain_attn, gain_ffn):
    weights = tuple((weight_arg.astype(jnp.float32) for weight_arg in (w_query, w_key, w_value, w_out, w_gate, w_up, w_down, gain_attn, gain_ffn)))
    buckets = tokens.shape[0] * tokens.shape[1]
    flat_tokens = tokens.reshape(buckets, BUCKET, D)
    flat_cotangent = cotangent.reshape(buckets, BUCKET, D)
    flat_lengths = lengths.reshape(buckets, PACK)

    def bucket_step(running, bucket_item):
        rows_in, upstream, lengths_row = bucket_item
        offset, live_mask, allowed = segment_tables(lengths_row, BUCKET)
        cosines, sines = rope_tables(offset, HD)
        tables = (cosines, sines, allowed)

        def forward(rows, params):
            first_out = block_pass(rows, params, tables)
            return block_pass(first_out, params, tables) * live_mask[:, None]
        result, pullback = jax.vjp(forward, rows_in.astype(jnp.float32), weights)
        d_rows, d_params = pullback(upstream.astype(jnp.float32))
        running = jax.tree.map(jnp.add, running, d_params)
        return (running, (result.astype(jnp.bfloat16), d_rows))
    zero_sums = jax.tree.map(jnp.zeros_like, weights)
    grad_sums, (outputs, input_grads) = lax.scan(bucket_step, zero_sums, (flat_tokens, flat_cotangent, flat_lengths))
    return (outputs.reshape(tokens.shape), input_grads.reshape(tokens.shape), grad_sums[0], grad_sums[1], grad_sums[2], grad_sums[3], grad_sums[4], grad_sums[5], grad_sums[6], grad_sums[7], grad_sums[8])
```

```python
import functools
import math

import jax
import jax.numpy as jnp
from jax import lax
from jax.experimental import pallas as pl
from jax.experimental.pallas import tpu as pltpu
from jax.sharding import PartitionSpec as P

HEADS = 9
KV_HEADS = 3
HD = 64
MESH = pl.DeviceIdType.MESH
F32 = jnp.float32
BF16 = jnp.bfloat16

WAVES = 4
STREAMS = 3
TILE_ROWS = 288


def segment_tables(lengths, count):
    bounds = jnp.cumsum(lengths, axis=-1)
    places = jnp.arange(count, dtype=jnp.int32)
    segment = jnp.sum((places[None, :, None] >= bounds[:, None, :]).astype(jnp.int32), axis=2)
    starts = jnp.concatenate([jnp.zeros_like(bounds[:, :1]), bounds], axis=1)
    matches = segment[:, :, None] == jnp.arange(starts.shape[1], dtype=jnp.int32)
    seg_begin = jnp.sum(jnp.where(matches, starts[:, None, :], 0), axis=2)
    offset = places[None] - seg_begin
    live_mask = (places[None] < bounds[:, -1:]).astype(F32)
    allowed = (segment[:, :, None] == segment[:, None, :]) & (
        places[None, None, :] <= places[None, :, None]
    )
    return (offset, live_mask, allowed)


def rope_tables(offset, head_dim):
    half_dim = head_dim // 2
    inverse = jnp.exp(
        jnp.arange(half_dim, dtype=F32) * (-2.0 * math.log(10000.0) / head_dim)
    )
    angles = offset.astype(F32)[..., None] * inverse
    return (jnp.cos(angles)[:, :, None, :], jnp.sin(angles)[:, :, None, :])


def rotate(values, cosines, sines):
    half_dim = values.shape[-1] // 2
    lower_half = values[..., :half_dim]
    upper_half = values[..., half_dim:]
    return jnp.concatenate(
        [lower_half * cosines - upper_half * sines, upper_half * cosines + lower_half * sines],
        axis=-1,
    )


def rms_norm(rows, gain):
    return rows * lax.rsqrt(jnp.mean(rows * rows, axis=-1, keepdims=True) + 1e-05) * gain


def dot(eq, a, b):
    return jnp.einsum(eq, a, b, preferred_element_type=F32)


def block_forward(rows, weights, tables, batch):
    w_query, w_key, w_value, w_out, w_gate, w_up, w_down, gain_attn, gain_ffn = weights
    cosines, sines, allowed = tables
    total = rows.shape[0]
    count = total // batch
    normed_one = rms_norm(rows, gain_attn.astype(F32)).astype(BF16)
    query = rotate(
        dot("sd,da->sa", normed_one, w_query).reshape(batch, count, HEADS, HD), cosines, sines
    ).astype(BF16)
    key = rotate(
        dot("sd,da->sa", normed_one, w_key).reshape(batch, count, KV_HEADS, HD), cosines, sines
    ).astype(BF16)
    value = dot("sd,da->sa", normed_one, w_value).reshape(batch, count, KV_HEADS, HD).astype(BF16)
    grouped = query.reshape(batch, count, KV_HEADS, HEADS // KV_HEADS, HD)
    scores = dot("bqkgd,bpkd->bkgqp", grouped, key) * (1.0 / math.sqrt(HD))
    scores = jnp.where(allowed[:, None, None], scores, -1000000000.0)
    probs = jax.nn.softmax(scores, axis=-1)
    mixed = dot("bkgqp,bpkd->bqkgd", probs.astype(BF16), value)
    attn_out = mixed.reshape(total, HEADS * HD).astype(BF16)
    middle = rows + dot("sa,ad->sd", attn_out, w_out)
    normed_two = rms_norm(middle, gain_ffn.astype(F32)).astype(BF16)
    gate_out = dot("sd,df->sf", normed_two, w_gate)
    up_out = dot("sd,df->sf", normed_two, w_up)
    hidden = (jax.nn.silu(gate_out) * up_out).astype(BF16)
    result = middle + dot("sf,fd->sd", hidden, w_down)
    saved = (
        rows, normed_one, grouped, key, value, attn_out, probs, middle, normed_two, gate_out, up_out, hidden,
    )
    return (result, saved)


def block_backward(upstream, saved, weights, tables, batch):
    w_query, w_key, w_value, w_out, w_gate, w_up, w_down, gain_attn, gain_ffn = weights
    cosines, sines, allowed = tables
    (
        rows, normed_one, grouped, key, value, attn_out, probs, middle, normed_two, gate_out, up_out, hidden,
    ) = saved
    total = rows.shape[0]
    count = total // batch
    scale_factor = 1.0 / math.sqrt(HD)
    d_down = upstream.astype(BF16)
    grad_down = dot("sf,sd->df", hidden, d_down)
    d_hidden = dot("sd,fd->sf", d_down, w_down)
    sigmoid_gate = jax.nn.sigmoid(gate_out)
    d_up = (d_hidden * (gate_out * sigmoid_gate)).astype(BF16)
    d_gate = (d_hidden * up_out * sigmoid_gate * (1.0 + gate_out * (1.0 - sigmoid_gate))).astype(
        BF16
    )
    grad_gate = dot("sd,sf->df", normed_two, d_gate)
    grad_up = dot("sd,sf->df", normed_two, d_up)
    d_normed_two = dot("sf,df->sd", d_gate, w_gate) + dot("sf,df->sd", d_up, w_up)
    unused_two, norm_pull_two = jax.vjp(rms_norm, middle, gain_ffn.astype(F32))
    d_middle_norm, grad_gain_ffn = norm_pull_two(d_normed_two)
    d_middle = upstream + d_middle_norm
    d_branch = d_middle.astype(BF16)
    grad_out = dot("sa,sd->ad", attn_out, d_branch)
    d_attn = dot("sd,ad->sa", d_branch, w_out).astype(BF16)
    d_grouped = d_attn.reshape(grouped.shape)
    d_probs = dot("bqkgd,bpkd->bkgqp", d_grouped, value)
    row_delta = jnp.sum(d_probs * probs, axis=-1, keepdims=True)
    d_scores = (probs * (d_probs - row_delta)).astype(BF16)
    d_query = dot("bkgqp,bpkd->bqkgd", d_scores, key) * scale_factor
    d_key = dot("bkgqp,bqkgd->bpkd", d_scores, grouped) * scale_factor
    d_value = dot("bkgqp,bqkgd->bpkd", probs.astype(BF16), d_grouped)
    d_query = d_query.reshape(batch, count, HEADS, HD)
    d_query_raw = rotate(d_query, cosines, -sines).reshape(total, -1).astype(BF16)
    d_key_raw = rotate(d_key, cosines, -sines).reshape(total, -1).astype(BF16)
    d_value_raw = d_value.reshape(total, -1).astype(BF16)
    grad_query = dot("sd,sa->da", normed_one, d_query_raw)
    grad_key = dot("sd,sa->da", normed_one, d_key_raw)
    grad_value = dot("sd,sa->da", normed_one, d_value_raw)
    d_normed_one = (
        dot("sa,da->sd", d_query_raw, w_query)
        + dot("sa,da->sd", d_key_raw, w_key)
        + dot("sa,da->sd", d_value_raw, w_value)
    )
    unused_one, norm_pull_one = jax.vjp(rms_norm, rows, gain_attn.astype(F32))
    d_rows_norm, grad_gain_attn = norm_pull_one(d_normed_one)
    grads = (
        grad_query, grad_key, grad_value, grad_out, grad_gate, grad_up, grad_down, grad_gain_attn, grad_gain_ffn,
    )
    return (d_middle + d_rows_norm, grads)


def stream_bits(wave, stream, bits):
    if stream == 0:
        return (0, 1, 2)
    if stream == 1:
        return (1, 0, 2)
    return (2, 0, 1) if wave % 2 == 0 else (2, 1, 0)


def reduce_kernel(
    bits, packed_ref, gain_ref, res_ref, gain_out_ref,
    acc, half_in, in1, in2, in3, in4, gain_buf,
    half_send, half_recv, send_sem, recv_sem, gain_send, gain_recv,
):
    dp = lax.axis_index("dp")
    core = lax.axis_index("fsdp")
    other = 1 - core
    value = [(dp // (1 << b)) % 2 for b in range(bits)]
    partner = [dp + (1 << b) * (1 - 2 * value[b]) for b in range(bits)]
    targets = [(dp, other)] + [(partner[b], core) for b in range(bits)]

    barrier = pltpu.get_barrier_semaphore()
    for target in targets:
        pl.semaphore_signal(barrier, inc=1, device_id=target, device_id_type=MESH)
    pl.semaphore_wait(barrier, len(targets))

    def remote(src, dst, send, recv, target):
        return pltpu.make_async_remote_copy(
            src_ref=src, dst_ref=dst, send_sem=send, recv_sem=recv, device_id=target,
            device_id_type=MESH,
        )

    started = []

    def start(copy):
        copy.start()
        started.append(copy)
        return copy

    tiles = 4 * STREAMS
    halves = [
        start(
            remote(
                packed_ref.at[other, pl.ds(w * tiles, tiles)],
                half_in.at[pl.ds(w * tiles, tiles)],
                half_send.at[w],
                half_recv.at[w],
                (dp, other),
            )
        )
        for w in range(WAVES)
    ]
    gain_steps = [((dp, other), None)] + [((partner[b], core), b) for b in range(bits)]
    gain_copies = []

    def gain_start(i):
        src = gain_ref.at[other] if i == 0 else gain_buf.at[0, i - 1]
        gain_copies.append(
            start(remote(src, gain_buf.at[1, i], gain_send.at[i], gain_recv.at[i], gain_steps[i][0]))
        )

    def gain_finish(i):
        gain_copies[i].wait_recv()
        own = gain_ref[core] if i == 0 else gain_buf[0, i - 1]
        gain_buf[0, i] = own + gain_buf[1, i]

    flight = {}
    steps = 4 + bits - 3 + 3
    half_rows = TILE_ROWS // 2

    def kept(w, s):
        b1, b2, b3 = stream_bits(w, s, bits)
        base = w * tiles + 4 * s
        two = base + 2 * value[b1]
        one = two + value[b2]
        rows = pl.multiple_of(half_rows * value[b3], 16)
        return base, two, one, rows, (b1, b2, b3)

    def do(w, s, step):
        base, two, one, rows, (b1, b2, b3) = kept(w, s)
        slot = w * STREAMS + s

        def go(src, dst, bit):
            flight[(w, s, step)] = start(
                remote(
                    src, dst, send_sem.at[slot, step], recv_sem.at[slot, step], (partner[bit], core)
                )
            )

        if step > 0:
            flight[(w, s, step - 1)].wait_recv()
        if step == 0:
            acc[pl.ds(base, 4)] = (
                packed_ref[core, pl.ds(base, 4)].astype(F32) + half_in[pl.ds(base, 4)].astype(F32)
            ).astype(BF16)
            go(acc.at[pl.ds(base + 2 * (1 - value[b1]), 2)], in1.at[slot], b1)
        elif step == 1:
            acc[pl.ds(two, 2)] = (acc[pl.ds(two, 2)].astype(F32) + in1[slot].astype(F32)).astype(BF16)
            go(acc.at[two + 1 - value[b2]], in2.at[slot], b2)
        elif step == 2:
            acc[one] = (acc[one].astype(F32) + in2[slot].astype(F32)).astype(BF16)
            away = pl.multiple_of(half_rows * (1 - value[b3]), 16)
            go(acc.at[one, pl.ds(away, half_rows)], in3.at[slot], b3)
        elif step < bits + 1:
            at = step - 3
            own = acc[one, pl.ds(rows, half_rows)] if at == 0 else in4[slot, 0, at - 1]
            came = in3[slot] if at == 0 else in4[slot, 1, at - 1]
            total = (own.astype(F32) + came.astype(F32)).astype(BF16)
            if step < bits:
                in4[slot, 0, at] = total
                go(in4.at[slot, 0, at], in4.at[slot, 1, at], step)
            else:
                here = res_ref.at[one, pl.ds(rows, half_rows)]
                res_ref[one, pl.ds(rows, half_rows)] = total
                go(here, here, b3)
        elif step == bits + 1:
            go(res_ref.at[one], res_ref.at[one], b2)
        elif step == bits + 2:
            go(res_ref.at[pl.ds(two, 2)], res_ref.at[pl.ds(two, 2)], b1)

    last = bits + 3
    gain_start(0)
    for diagonal in range(WAVES + last):
        if diagonal <= bits:
            gain_finish(diagonal)
            if diagonal < bits:
                gain_start(diagonal + 1)
        for w in range(WAVES):
            step = diagonal - w
            if step == 0:
                halves[w].wait_recv()
            if 0 <= step <= last:
                for s in range(STREAMS):
                    do(w, s, step)
    gain_out_ref[...] = gain_buf[0, bits]
    for copy in started:
        copy.wait_send()


def all_reduce(packed, gains, bits):
    slots = WAVES * STREAMS
    half = (TILE_ROWS // 2, 128)
    steps = bits + 3
    vmem = pl.BlockSpec(memory_space=pltpu.VMEM)
    return pl.pallas_call(
        functools.partial(reduce_kernel, bits),
        out_shape=(
            jax.ShapeDtypeStruct(packed.shape[1:], BF16),
            jax.ShapeDtypeStruct(gains.shape[1:], F32),
        ),
        in_specs=[vmem, vmem],
        out_specs=(vmem, vmem),
        scratch_shapes=[
            pltpu.VMEM(packed.shape[1:], BF16),
            pltpu.VMEM(packed.shape[1:], BF16),
            pltpu.VMEM((slots, 2, TILE_ROWS, 128), BF16),
            pltpu.VMEM((slots, TILE_ROWS, 128), BF16),
            pltpu.VMEM((slots, *half), BF16),
            pltpu.VMEM((slots, 2, bits - 3, *half), BF16),
            pltpu.VMEM((2, bits + 1, *gains.shape[1:]), F32),
            pltpu.SemaphoreType.DMA((WAVES,)),
            pltpu.SemaphoreType.DMA((WAVES,)),
            pltpu.SemaphoreType.DMA((slots, steps)),
            pltpu.SemaphoreType.DMA((slots, steps)),
            pltpu.SemaphoreType.DMA((bits + 1,)),
            pltpu.SemaphoreType.DMA((bits + 1,)),
        ],
        compiler_params=pltpu.CompilerParams(
            collective_id=0, has_side_effects=True, vmem_limit_bytes=48 << 20
        ),
    )(packed, gains)


def to_tiles(rows):
    return rows.reshape(2, TILE_ROWS, -1, 128).transpose(0, 2, 1, 3)


def on_device(
    bits, tokens, cotangent, lengths, w_query, w_key, w_value, w_out, w_gate, w_up, w_down, gain_attn, gain_ffn,
):
    batch, unused, count, width = tokens.shape
    weights = tuple(
        lax.all_gather(w, "fsdp", axis=0, tiled=True)
        for w in (w_query, w_key, w_value, w_out, w_gate, w_up, w_down, gain_attn, gain_ffn)
    )
    offset, live_mask, allowed = segment_tables(lengths[:, 0], count)
    cosines, sines = rope_tables(offset, HD)
    tables = (cosines, sines, allowed)
    live = live_mask.reshape(-1, 1)
    rows_in = tokens.reshape(batch * count, width).astype(F32)
    first_out, first_saved = block_forward(rows_in, weights, tables, batch)
    second_out, second_saved = block_forward(first_out, weights, tables, batch)
    output = (second_out * live).astype(BF16).reshape(tokens.shape)
    upstream = cotangent.reshape(batch * count, width).astype(F32) * live
    upstream, second_grads = block_backward(upstream, second_saved, weights, tables, batch)
    upstream, first_grads = block_backward(upstream, first_saved, weights, tables, batch)
    input_grad = upstream.reshape(tokens.shape)
    q, k, v, o, g, u, d, ga, gf = jax.tree.map(jnp.add, first_grads, second_grads)
    top = jnp.concatenate([g, u, q, k, v, o], axis=1).astype(BF16)
    ff = d.shape[1]
    down = d.astype(BF16).reshape(2, TILE_ROWS, 2, ff // 256, 128).transpose(2, 0, 3, 1, 4)
    packed = jnp.concatenate([down.reshape(2, -1, TILE_ROWS, 128), to_tiles(top)], axis=1)
    gains = jnp.concatenate([ga.reshape(2, -1), gf.reshape(2, -1)], axis=1)
    gains = jnp.pad(gains, ((0, 0), (0, 1024 - gains.shape[1]))).reshape(2, 8, 128)
    res, gain_sum = all_reduce(packed, gains, bits)
    res = res.astype(F32)
    nd = ff // 128
    down = res[:nd].reshape(2, ff // 256, TILE_ROWS, 128).transpose(1, 3, 0, 2)
    down = down.reshape(ff // 2, width)
    top = res[nd:].transpose(1, 0, 2).reshape(TILE_ROWS, -1)
    kv = KV_HEADS * HD
    sizes = [ff, ff, width, kv, kv, width]
    parts, at = [], 0
    for size in sizes:
        parts.append(top[:, at : at + size])
        at += size
    gg, gu, gq, gk, gv, go = parts
    gain_sum = gain_sum.reshape(-1)
    return (
        output, input_grad, gq, gk, gv, go, gg, gu, down,
        gain_sum[:TILE_ROWS], gain_sum[TILE_ROWS : 2 * TILE_ROWS],
    )


def solution(mesh):
    rows = P(None, ("dp", "fsdp"), None, None)
    weight = P("fsdp", None)
    in_specs = (rows, rows, P(None, ("dp", "fsdp"), None)) + (weight,) * 7 + (P("fsdp"),) * 2
    out_specs = (rows, rows) + (weight,) * 7 + (P("fsdp"),) * 2
    bits = mesh.shape["dp"].bit_length() - 1
    return jax.shard_map(
        functools.partial(on_device, bits),
        mesh=mesh,
        in_specs=in_specs,
        out_specs=out_specs,
        check_vma=False,
    )
```

```python
import functools
import math

import jax
import jax.numpy as jnp
import ml_dtypes
import numpy as np
from jax import lax
from jax.experimental import pallas as pl
from jax.experimental.pallas import tpu as pltpu
from jax.sharding import PartitionSpec as P

HEADS = 9
KV_HEADS = 3
GROUP = HEADS // KV_HEADS
HD = 64
D = 576
FF = 1536
KVW = KV_HEADS * HD
BUCKET = 128
MESH = pl.DeviceIdType.MESH
F32 = jnp.float32
BF16 = jnp.bfloat16

WAVES = 4
STREAMS = 3
TILES = 4 * STREAMS
TILE_ROWS = 288
QKV = 1024
CHUNK = 256


def nn(a, b):
    return lax.dot_general(a, b, (((1,), (0,)), ((), ())), preferred_element_type=F32)


def nt(a, b):
    return lax.dot_general(a, b, (((1,), (1,)), ((), ())), preferred_element_type=F32)


def tn(a, b):
    return lax.dot_general(a, b, (((0,), (0,)), ((), ())), preferred_element_type=F32)


def cols(c, size=CHUNK):
    return pl.ds(pl.multiple_of(c * size, size), size)


def rope_table():
    lane = np.arange(128)
    inverse = np.exp((lane % 32) * (-2.0 * math.log(10000.0) / HD))
    angles = np.arange(BUCKET)[:, None] * inverse[None, :]
    sign = np.where(lane % 64 < 32, -1.0, 1.0)
    rest = np.concatenate([np.cos(angles), np.sin(angles) * sign], axis=1)
    parts = []
    for unused in range(3):
        part = rest.astype(ml_dtypes.bfloat16)
        parts.append(part)
        rest = rest - part.astype(np.float64)
    return np.concatenate(parts, axis=1)


def stream_bits(wave, stream):
    if stream == 0:
        return (0, 1, 2)
    if stream == 1:
        return (1, 0, 2)
    return (2, 0, 1) if wave % 2 == 0 else (2, 1, 0)


def remote(src, dst, send, recv, target):
    return pltpu.make_async_remote_copy(
        src_ref=src, dst_ref=dst, send_sem=send, recv_sem=recv, device_id=target,
        device_id_type=MESH,
    )


class Reduction:
    def __init__(self, bits, dp, core, packed, res, ins, gain_buf, sems):
        self.bits, self.core, self.packed, self.res = bits, core, packed, res
        self.in1, self.in2, self.in3, self.in4 = ins
        self.gain_buf = gain_buf
        (
            self.half_send, self.half_recv, self.send_sem, self.recv_sem, self.gain_send, self.gain_recv,
        ) = sems
        self.value = [(dp // (1 << b)) % 2 for b in range(bits)]
        self.partner = [dp + (1 << b) * (1 - 2 * self.value[b]) for b in range(bits)]
        self.mate = (dp, 1 - core)
        self.targets = [self.mate] + [(self.partner[b], core) for b in range(bits)]
        self.last = bits + 3
        self.started, self.flight, self.halves, self.gain_copies = [], {}, {}, []

    def start(self, copy):
        copy.start()
        self.started.append(copy)
        return copy

    def exchange(self, w):
        tiles = pl.ds(w * TILES, TILES)
        self.halves[w] = remote(
            self.packed.at[1 - self.core, tiles], self.res.at[tiles],
            self.half_send.at[w], self.half_recv.at[w], self.mate,
        )
        self.halves[w].start()

    def gain_start(self, i):
        target = self.targets[i]
        self.gain_copies.append(
            self.start(
                remote(
                    self.gain_buf.at[0, i], self.gain_buf.at[1, i], self.gain_send.at[i],
                    self.gain_recv.at[i], target,
                )
            )
        )

    def gain_finish(self, i):
        self.gain_copies[i].wait_recv()
        self.gain_buf[0, i + 1] = self.gain_buf[0, i] + self.gain_buf[1, i]

    def step(self, w, step):
        if step == 0:
            self.halves[w].wait()
        for s in range(STREAMS):
            self.stream_step(w, s, step)

    def stream_step(self, w, s, step):
        value, core, packed, res = self.value, self.core, self.packed, self.res
        b1, b2, b3 = stream_bits(w, s)
        base = w * TILES + 4 * s
        two = base + 2 * value[b1]
        one = two + value[b2]
        half = TILE_ROWS // 2
        rows = pl.ds(pl.multiple_of(half * value[b3], 16), half)
        slot = w * STREAMS + s

        def go(src, dst, bit):
            self.flight[(slot, step)] = self.start(
                remote(
                    src, dst, self.send_sem.at[slot, step], self.recv_sem.at[slot, step],
                    (self.partner[bit], core),
                )
            )

        if step > 0:
            self.flight[(slot, step - 1)].wait_recv()
        if step == 0:
            for t in range(4):
                packed[core, base + t] = (
                    packed[core, base + t].astype(F32) + res[base + t].astype(F32)
                ).astype(BF16)
            go(packed.at[core, pl.ds(base + 2 * (1 - value[b1]), 2)], self.in1.at[slot], b1)
        elif step == 1:
            for t in range(2):
                packed[core, two + t] = (
                    packed[core, two + t].astype(F32) + self.in1[slot, t].astype(F32)
                ).astype(BF16)
            go(packed.at[core, two + 1 - value[b2]], self.in2.at[slot], b2)
        elif step == 2:
            packed[core, one] = (
                packed[core, one].astype(F32) + self.in2[slot].astype(F32)
            ).astype(BF16)
            away = pl.ds(pl.multiple_of(half * (1 - value[b3]), 16), half)
            go(packed.at[core, one, away], self.in3.at[slot], b3)
        elif step < self.bits + 1:
            at = step - 3
            own = packed[core, one, rows] if at == 0 else self.in4[slot, 0, at - 1]
            came = self.in3[slot] if at == 0 else self.in4[slot, 1, at - 1]
            total = (own.astype(F32) + came.astype(F32)).astype(BF16)
            if step < self.bits:
                self.in4[slot, 0, at] = total
                go(self.in4.at[slot, 0, at], self.in4.at[slot, 1, at], step)
            else:
                res[one, rows] = total
                go(res.at[one, rows], res.at[one, rows], b3)
        elif step == self.bits + 1:
            go(res.at[one], res.at[one], b2)
        elif step == self.bits + 2:
            go(res.at[pl.ds(two, 2)], res.at[pl.ds(two, 2)], b1)


def layer_kernel(
    bits, buckets,
    lengths_ref, tokens_ref, cot_ref, wq_ref, wk_ref, wv_ref, wo_ref, wg_ref, wu_ref, wd_ref, gain_ref, table_ref,
    out_ref, dx_ref, res_ref, gain_out_ref,
    wqkv, wo, wg, wu, wd, gain_in, gain_own, cs, bias,
    norm, norm_t1, norm_t2, att, att_t, down_t, qk, val, probs, x_two, middle, hidden, d_up, d_gate,
    grad, dn, d_branch, d_qkv, packed, in1, in2, in3, in4, gain_buf,
    w_send, w_recv, w_local, half_send, half_recv, send_sem, recv_sem, gain_send, gain_recv,
):
    dp = lax.axis_index("dp")
    core = lax.axis_index("fsdp")
    total = buckets * BUCKET
    red = Reduction(
        bits, dp, core, packed, res_ref, (in1, in2, in3, in4), gain_buf,
        (half_send, half_recv, send_sem, recv_sem, gain_send, gain_recv),
    )
    barrier = pltpu.get_barrier_semaphore()
    for target in red.targets:
        pl.semaphore_signal(barrier, inc=1, device_id=target, device_id_type=MESH)

    half = pl.ds(pl.multiple_of(core * TILE_ROWS, 16), TILE_ROWS)
    down_half = pl.ds(pl.multiple_of(core * (FF // 2), 16), FF // 2)
    wqkv[half, :] = jnp.concatenate(
        [
            (wq_ref[...].astype(F32) * (1.0 / math.sqrt(HD))).astype(BF16),
            wk_ref[...],
            wv_ref[...],
            jnp.zeros((TILE_ROWS, QKV - D - 2 * KVW), BF16),
        ],
        axis=1,
    )
    gain_own[...] = gain_ref[...]
    pl.semaphore_wait(barrier, len(red.targets))

    whole = [
        (wqkv.at[half], wqkv.at[half]), (wo_ref, wo.at[half]), (wg_ref, wg.at[half]),
        (wu_ref, wu.at[half]), (wd_ref, wd.at[down_half]), (gain_own, gain_in),
    ]
    arrivals, locals_ = [], []
    for i, (src, dst) in enumerate(whole):
        arrivals.append(red.start(remote(src, dst, w_send.at[i], w_recv.at[i], red.mate)))
        if 1 <= i <= 4:
            copy = pltpu.make_async_copy(src, dst, w_local.at[i - 1])
            copy.start()
            locals_.append(copy)

    def weight(i):
        if i >= 1:
            locals_[i - 1].wait()
        arrivals[i].wait_recv()

    lane = lax.broadcasted_iota(jnp.int32, (BUCKET, BUCKET), 1)
    place = lax.broadcasted_iota(jnp.int32, (BUCKET, BUCKET), 0)
    first_half = lane % HD < HD // 2

    def bucket_rows(b):
        return pl.ds(pl.multiple_of(b * BUCKET, BUCKET), BUCKET)

    def shifted(rows, by):
        return pl.ds(pl.multiple_of(rows.start + by, BUCKET), BUCKET)

    def make_tables(b, carry):
        begin = jnp.zeros((BUCKET, BUCKET), jnp.int32)
        bound = 0
        for j in range(lengths_ref.shape[1]):
            bound = bound + lengths_ref[b, j]
            begin = begin + jnp.where(place >= bound, lengths_ref[b, j], 0)
        pick = jnp.where(place - begin == lane, 1.0, 0.0).astype(BF16)
        size = table_ref.shape[1] // 3
        cs[bucket_rows(b), :] = (
            nn(pick, table_ref[:, :size])
            + nn(pick, table_ref[:, size : 2 * size])
            + nn(pick, table_ref[:, 2 * size :])
        )
        bias[b] = jnp.where((lane >= begin) & (lane <= place), 0.0, -1e30)
        return carry

    lax.fori_loop(0, buckets, make_tables, 0)

    def live(b):
        bound = 0
        for j in range(lengths_ref.shape[1]):
            bound = bound + lengths_ref[b, j]
        row = lax.broadcasted_iota(jnp.int32, (BUCKET, 1), 0)
        return (row < bound).astype(F32)

    def rope(x, cosines, sines, sign):
        turned = jnp.where(
            lax.broadcasted_iota(jnp.int32, x.shape, 1) % HD < HD // 2,
            pltpu.roll(x, 128 - HD // 2, 1),
            pltpu.roll(x, HD // 2, 1),
        )
        if sign > 0:
            return x * cosines + turned * sines
        return x * cosines - turned * sines

    arrivals[5].wait_recv()
    wide = lax.broadcasted_iota(jnp.int32, (8, 640), 1)
    low_half = jnp.where(core == 0, gain_own[...], gain_in[...])
    high_half = jnp.where(core == 0, gain_in[...], gain_own[...])
    gains = jnp.where(wide < TILE_ROWS, low_half, pltpu.roll(high_half, TILE_ROWS, 1))
    gain_attn, gain_ffn = gains[0:1, :D], gains[1:2, :D]
    gain_buf[0, 0] = jnp.zeros((8, 640), F32)

    def inverse_rms(x):
        return lax.rsqrt(jnp.mean(x * x, axis=-1, keepdims=True) + 1e-05)

    def norm_forward(p, read, gain, norm_t):
        def body(b, carry):
            x = read(bucket_rows(b))
            n = (x * inverse_rms(x) * gain).astype(BF16)
            norm[bucket_rows(b), :] = n
            norm_t[:, bucket_rows(p * buckets + b)] = n.T
            return carry

        lax.fori_loop(0, buckets, body, 0)

    def norm_backward(read, gain, row):
        def body(b, carry):
            rows = bucket_rows(b)
            x = read(rows)
            inv = inverse_rms(x)
            hat = x * inv
            d = dn[rows, :]
            dg = d * gain
            grad[rows, :] = grad[rows, :] + inv * (
                dg - hat * jnp.mean(dg * hat, axis=-1, keepdims=True)
            )
            gain_buf[0, 0, row : row + 1, :D] = gain_buf[0, 0, row : row + 1, :D] + jnp.sum(
                d * hat, axis=0, keepdims=True
            )
            return carry

        lax.fori_loop(0, buckets, body, 0)

    def read_x(p):
        if p == 0:
            return lambda rows: tokens_ref[rows, :].astype(F32)
        return lambda rows: x_two[rows, :]

    def forward(p):
        at = pl.ds(p * total, total)
        norm_forward(p, read_x(p), gain_attn, norm_t1)
        if p == 0:
            weight(0)
        for c in range(QKV // CHUNK):
            z = nn(norm[...], wqkv[:, c * CHUNK : (c + 1) * CHUNK])
            if c < 3:
                for j in range(2):
                    lanes = slice(c * CHUNK + 128 * j, c * CHUNK + 128 * (j + 1))
                    qk[at, lanes] = rope(
                        z[:, 128 * j : 128 * (j + 1)], cs[:, :128], cs[:, 128:], 1
                    ).astype(BF16)
            else:
                val[at, :] = z.astype(BF16)

        def attend(b, carry):
            rows = bucket_rows(p * buckets + b)
            outs = []
            for g in range(KV_HEADS):
                key = qk[rows, D + HD * g : D + HD * (g + 1)]
                query = jnp.concatenate(
                    [qk[rows, HD * h : HD * (h + 1)] for h in range(GROUP * g, GROUP * (g + 1))],
                    axis=0,
                )
                scores = nt(query, key) + jnp.concatenate([bias[b]] * GROUP, axis=0)
                e = jnp.exp(scores - jnp.max(scores, axis=-1, keepdims=True))
                low = (e * (1.0 / jnp.sum(e, axis=-1, keepdims=True))).astype(BF16)
                probs[p * buckets + b, g] = low
                mixed = nn(low, val[rows, HD * g : HD * (g + 1)]).astype(BF16)
                outs += [mixed[BUCKET * i : BUCKET * (i + 1)] for i in range(GROUP)]
            out = jnp.concatenate(outs, axis=1)
            att[bucket_rows(b), :] = out
            att_t[:, rows] = out.T
            return carry

        lax.fori_loop(0, buckets, attend, 0)
        if p == 0:
            weight(1)
        mixed = nn(att[...], wo[...])
        middle[at, :] = (tokens_ref[...].astype(F32) if p == 0 else x_two[...]) + mixed
        norm_forward(p, lambda rows: middle[shifted(rows, p * total), :], gain_ffn, norm_t2)
        if p == 0:
            weight(2)
            weight(3)

        def gated(c, carry):
            gate = nn(norm[...], wg[:, cols(c)])
            up = nn(norm[...], wu[:, cols(c)])
            s = 1.0 / (1.0 + jnp.exp(-gate))
            silu = gate * s
            hidden[at, cols(c)] = (silu * up).astype(BF16)
            d_up[at, cols(c)] = silu.astype(BF16)
            d_gate[at, cols(c)] = (up * (s + silu * (1.0 - s))).astype(BF16)
            return carry

        lax.fori_loop(0, FF // CHUNK, gated, 0)
        if p == 0:
            weight(4)
        result = middle[at, :] + nn(hidden[at, :], wd[...])
        if p == 0:
            x_two[...] = result
        else:
            for b in range(buckets):
                rows = slice(b * BUCKET, (b + 1) * BUCKET)
                mask = live(b)
                out_ref[rows, :] = (result[rows] * mask).astype(BF16)
                grad[rows, :] = cot_ref[rows, :].astype(F32) * mask

    def put(first, block):
        low = block.astype(BF16)
        for h in range(2):
            for j in range(2):
                packed[h, first + j] = low[
                    TILE_ROWS * h : TILE_ROWS * (h + 1), 128 * j : 128 * (j + 1)
                ]

    def grad_down(c, carry):
        low = nn(down_t[...], hidden[:, cols(c)]).astype(BF16)
        per = FF // 2 // CHUNK
        for h in range(2):
            for j in range(2):
                packed[c // per, 6 * h + 2 * (c % per) + j] = low[
                    TILE_ROWS * h : TILE_ROWS * (h + 1), 128 * j : 128 * (j + 1)
                ]
        return carry

    def backward(p):
        at = pl.ds(p * total, total)
        low = grad[...].astype(BF16)
        norm[...] = low
        down_t[:, at] = low.T
        if p == 0:
            lax.fori_loop(0, FF // CHUNK, grad_down, 0)
            red.exchange(0)

        def gated(c, carry):
            d_hidden = nt(norm[...], wd[cols(c), :])
            d_up[at, cols(c)] = (d_hidden * d_up[at, cols(c)].astype(F32)).astype(BF16)
            d_gate[at, cols(c)] = (d_hidden * d_gate[at, cols(c)].astype(F32)).astype(BF16)
            return carry

        lax.fori_loop(0, FF // CHUNK, gated, 0)
        if p == 0:

            def grad_gate(c, carry):
                put(TILES + 2 * c, nn(norm_t2[...], d_gate[:, cols(c)]))
                return carry

            def grad_up(c, carry):
                put(2 * TILES + 2 * c, nn(norm_t2[...], d_up[:, cols(c)]))
                return carry

            lax.fori_loop(0, FF // CHUNK, grad_gate, 0)
            red.exchange(1)
            lax.fori_loop(0, FF // CHUNK, grad_up, 0)
            red.exchange(2)
        dn[...] = nt(d_gate[at, :], wg[...]) + nt(d_up[at, :], wu[...])
        norm_backward(lambda rows: middle[shifted(rows, p * total), :], gain_ffn, 1)
        low = grad[...].astype(BF16)
        d_branch[at, :] = low
        att[...] = nt(low, wo[...]).astype(BF16)

        def attend(b, carry):
            rows = bucket_rows(p * buckets + b)
            here = bucket_rows(b)
            d_query, d_key, d_value = [], [], []
            for g in range(KV_HEADS):
                heads = range(GROUP * g, GROUP * (g + 1))
                key = qk[rows, D + HD * g : D + HD * (g + 1)]
                query = jnp.concatenate([qk[rows, HD * h : HD * (h + 1)] for h in heads], axis=0)
                d_att = jnp.concatenate([att[here, HD * h : HD * (h + 1)] for h in heads], axis=0)
                low = probs[p * buckets + b, g]
                pr = low.astype(F32)
                dp_ = nt(d_att, val[rows, HD * g : HD * (g + 1)])
                ds = (pr * (dp_ - jnp.sum(dp_ * pr, axis=-1, keepdims=True))).astype(BF16)
                dq = nn(ds, key)
                d_query += [dq[BUCKET * i : BUCKET * (i + 1)] for i in range(GROUP)]
                d_key.append(tn(ds, query))
                d_value.append(tn(low, d_att))
            raw = jnp.concatenate(d_query + d_key, axis=1)
            for j in range((D + KVW) // 128):
                lanes = slice(128 * j, 128 * (j + 1))
                d_qkv[rows, lanes] = rope(
                    raw[:, lanes], cs[here, :128], cs[here, 128:], -1
                ).astype(BF16)
            d_qkv[rows, D + KVW :] = jnp.concatenate(
                d_value + [jnp.zeros((BUCKET, QKV - D - 2 * KVW), F32)], axis=1
            ).astype(BF16)
            return carry

        lax.fori_loop(0, buckets, attend, 0)
        dn[...] = nt(d_qkv[at, :], wqkv[...])
        norm_backward(read_x(p), gain_attn, 0)

    forward(0)
    forward(1)
    backward(1)
    backward(0)
    dx_ref[...] = grad[...]
    red.gain_start(0)

    lane_row = lax.broadcasted_iota(jnp.int32, (1, CHUNK), 1)
    scale = 1.0 / math.sqrt(HD)
    for c in range(3):
        block = nn(norm_t1[...], d_qkv[:, c * CHUNK : (c + 1) * CHUNK])
        put(3 * TILES + 2 * c, block * jnp.where(lane_row + c * CHUNK < D, scale, 1.0))
    block = nn(norm_t1[...], d_qkv[:, 3 * CHUNK :])
    rest = nn(att_t[...], d_branch[:, 2 * CHUNK :])
    put(3 * TILES + 6, jnp.concatenate([block[:, : D + 2 * KVW - 3 * CHUNK], rest], axis=1))
    for c in range(2):
        put(3 * TILES + 8 + 2 * c, nn(att_t[...], d_branch[:, c * CHUNK : (c + 1) * CHUNK]))
    red.exchange(3)

    for diagonal in range(WAVES + red.last):
        if diagonal <= bits:
            red.gain_finish(diagonal)
            if diagonal < bits:
                red.gain_start(diagonal + 1)
        for w in range(WAVES):
            if 0 <= diagonal - w <= red.last:
                red.step(w, diagonal - w)
    sums = gain_buf[0, bits + 1]
    gain_out_ref[...] = jnp.where(core == 0, sums, pltpu.roll(sums, 640 - TILE_ROWS, 1))
    for copy in red.started:
        copy.wait_send()


def run_layer(bits, lengths, tokens, cotangent, weights, gains):
    total = tokens.shape[0]
    buckets = total // BUCKET
    slots = WAVES * STREAMS
    half = (TILE_ROWS // 2, 128)
    steps = bits + 3
    vmem = pl.BlockSpec(memory_space=pltpu.VMEM)
    hbm = pl.BlockSpec(memory_space=pl.ANY)
    dma = pltpu.SemaphoreType.DMA
    grads = (WAVES * TILES, TILE_ROWS, 128)
    scratch = [
        ((D, QKV), BF16), ((D, D), BF16), ((D, FF), BF16), ((D, FF), BF16), ((FF, D), BF16),
        ((8, 640), F32), ((8, 640), F32), ((total, 256), F32), ((buckets, BUCKET, BUCKET), F32),
        ((total, D), BF16), ((D, 2 * total), BF16), ((D, 2 * total), BF16),
        ((total, D), BF16), ((D, 2 * total), BF16), ((D, 2 * total), BF16),
        ((2 * total, D + KVW), BF16), ((2 * total, CHUNK), BF16),
        ((2 * buckets, KV_HEADS, GROUP * BUCKET, BUCKET), BF16),
        ((total, D), F32), ((2 * total, D), F32),
        ((2 * total, FF), BF16), ((2 * total, FF), BF16), ((2 * total, FF), BF16),
        ((total, D), F32), ((total, D), F32), ((2 * total, D), BF16), ((2 * total, QKV), BF16),
        ((2, *grads), BF16), ((slots, 2, TILE_ROWS, 128), BF16), ((slots, TILE_ROWS, 128), BF16),
        ((slots, *half), BF16), ((slots, 2, bits - 3, *half), BF16), ((2, bits + 2, 8, 640), F32),
    ]
    return pl.pallas_call(
        functools.partial(layer_kernel, bits, buckets),
        out_shape=(
            jax.ShapeDtypeStruct((total, D), BF16),
            jax.ShapeDtypeStruct((total, D), F32),
            jax.ShapeDtypeStruct(grads, BF16),
            jax.ShapeDtypeStruct((8, 640), F32),
        ),
        in_specs=[pl.BlockSpec(memory_space=pltpu.SMEM)] + [vmem] * 5 + [hbm] * 4 + [vmem] * 2,
        out_specs=(vmem,) * 4,
        scratch_shapes=[pltpu.VMEM(shape, dtype) for shape, dtype in scratch]
        + [
            dma((6,)), dma((6,)), dma((4,)), dma((WAVES,)), dma((WAVES,)), dma((slots, steps)),
            dma((slots, steps)), dma((bits + 1,)), dma((bits + 1,)),
        ],
        compiler_params=pltpu.CompilerParams(
            collective_id=0, has_side_effects=True, vmem_limit_bytes=63 << 20
        ),
    )(lengths, tokens, cotangent, *weights, gains, jnp.asarray(rope_table()))


def on_device(
    bits, tokens, cotangent, lengths, w_query, w_key, w_value, w_out, w_gate, w_up, w_down, gain_attn, gain_ffn,
):
    batch, unused, count, width = tokens.shape
    gains = jnp.stack([gain_attn, gain_ffn]).astype(F32)
    gains = jnp.pad(gains, ((0, 6), (0, 640 - TILE_ROWS)))
    output, input_grad, res, gain_sum = run_layer(
        bits,
        lengths[:, 0],
        tokens.reshape(batch * count, width),
        cotangent.reshape(batch * count, width),
        (w_query, w_key, w_value, w_out, w_gate, w_up, w_down),
        gains,
    )
    res = res.astype(F32)
    down = res[:TILES].reshape(2, FF // 256, TILE_ROWS, 128).transpose(1, 3, 0, 2)
    down = down.reshape(FF // 2, width)
    top = res[TILES:].transpose(1, 0, 2).reshape(TILE_ROWS, -1)
    base = 2 * FF
    out = base + QKV
    pieces = (
        top[:, base : base + D],
        top[:, base + D : base + D + KVW],
        top[:, base + D + KVW : base + D + 2 * KVW],
        jnp.concatenate([top[:, out : out + 512], top[:, base + D + 2 * KVW : out]], axis=1),
        top[:, :FF],
        top[:, FF : 2 * FF],
    )
    return (
        output.reshape(tokens.shape), input_grad.reshape(tokens.shape), *pieces, down,
        gain_sum[0, :TILE_ROWS], gain_sum[1, :TILE_ROWS],
    )


def solution(mesh):
    rows = P(None, ("dp", "fsdp"), None, None)
    weight = P("fsdp", None)
    in_specs = (rows, rows, P(None, ("dp", "fsdp"), None)) + (weight,) * 7 + (P("fsdp"),) * 2
    out_specs = (rows, rows) + (weight,) * 7 + (P("fsdp"),) * 2
    bits = mesh.shape["dp"].bit_length() - 1
    return jax.shard_map(
        functools.partial(on_device, bits),
        mesh=mesh,
        in_specs=in_specs,
        out_specs=out_specs,
        check_vma=False,
    )
```

```python
import functools
import math

import jax
import jax.numpy as jnp
import ml_dtypes
import numpy as np
from jax import lax
from jax.experimental import pallas as pl
from jax.experimental.pallas import tpu as pltpu
from jax.sharding import PartitionSpec as P

HEADS = 9
KV_HEADS = 3
GROUP = HEADS // KV_HEADS
HD = 64
D = 576
FF = 1536
KVW = KV_HEADS * HD
BUCKET = 128
MESH = pl.DeviceIdType.MESH
F32 = jnp.float32
BF16 = jnp.bfloat16

WAVES = 4
STREAMS = 3
TILES = 4 * STREAMS
TILE_ROWS = 288
QKV = 1024
CHUNK = 256


def nn(a, b):
    return lax.dot_general(a, b, (((1,), (0,)), ((), ())), preferred_element_type=F32)


def nt(a, b):
    return lax.dot_general(a, b, (((1,), (1,)), ((), ())), preferred_element_type=F32)


def tn(a, b):
    return lax.dot_general(a, b, (((0,), (0,)), ((), ())), preferred_element_type=F32)


def rope_table():
    inverse = np.exp(np.arange(HD // 2) * (-2.0 * math.log(10000.0) / HD))
    angles = inverse[:, None] * np.arange(BUCKET)[None, :]
    rest = np.concatenate([np.cos(angles), np.sin(angles)], axis=0)
    parts = []
    for unused in range(3):
        part = rest.astype(ml_dtypes.bfloat16)
        parts.append(part)
        rest = rest - part.astype(np.float64)
    return np.concatenate(parts, axis=0)


def stream_bits(wave, stream):
    if stream == 0:
        return (0, 1, 2)
    if stream == 1:
        return (1, 0, 2)
    return (2, 0, 1) if wave % 2 == 0 else (2, 1, 0)


def remote(src, dst, send, recv, target):
    return pltpu.make_async_remote_copy(
        src_ref=src, dst_ref=dst, send_sem=send, recv_sem=recv, device_id=target,
        device_id_type=MESH,
    )


class Reduction:
    def __init__(self, bits, dp, core, packed, res, ins, gain_buf, sems):
        self.bits, self.core, self.packed, self.res = bits, core, packed, res
        self.in1, self.in2, self.in3, self.in4 = ins
        self.gain_buf = gain_buf
        (
            self.half_send, self.half_recv, self.send_sem, self.recv_sem, self.gain_send, self.gain_recv,
        ) = sems
        self.value = [(dp // (1 << b)) % 2 for b in range(bits)]
        self.partner = [dp + (1 << b) * (1 - 2 * self.value[b]) for b in range(bits)]
        self.mate = (dp, 1 - core)
        self.targets = [self.mate] + [(self.partner[b], core) for b in range(bits)]
        self.last = bits + 3
        self.started, self.flight, self.halves, self.gain_copies = [], {}, {}, []
        self.done = set()

    def start(self, copy):
        copy.start()
        self.started.append(copy)
        return copy

    def exchange(self, w):
        tiles = pl.ds(w * TILES, TILES)
        self.halves[w] = remote(
            self.packed.at[1 - self.core, tiles], self.res.at[tiles],
            self.half_send.at[w], self.half_recv.at[w], self.mate,
        )
        self.halves[w].start()

    def gain_start(self, i):
        target = self.targets[i]
        self.gain_copies.append(
            self.start(
                remote(
                    self.gain_buf.at[0, i], self.gain_buf.at[1, i], self.gain_send.at[i],
                    self.gain_recv.at[i], target,
                )
            )
        )

    def gain_finish(self, i):
        self.gain_copies[i].wait_recv()
        self.gain_buf[0, i + 1] = self.gain_buf[0, i] + self.gain_buf[1, i]

    def step(self, w, step):
        if (w, step) in self.done:
            return
        self.done.add((w, step))
        if step == 0:
            self.halves[w].wait()
        for s in range(STREAMS):
            self.stream_step(w, s, step)

    def stream_step(self, w, s, step):
        value, core, packed, res = self.value, self.core, self.packed, self.res
        b1, b2, b3 = stream_bits(w, s)
        base = w * TILES + 4 * s
        two = base + 2 * value[b1]
        one = two + value[b2]
        half = TILE_ROWS // 2
        rows = pl.ds(pl.multiple_of(half * value[b3], 16), half)
        slot = w * STREAMS + s

        def go(src, dst, bit):
            self.flight[(slot, step)] = self.start(
                remote(
                    src, dst, self.send_sem.at[slot, step], self.recv_sem.at[slot, step],
                    (self.partner[bit], core),
                )
            )

        if step > 0:
            self.flight[(slot, step - 1)].wait_recv()
        if step == 0:
            for t in range(4):
                packed[core, base + t] = (
                    packed[core, base + t].astype(F32) + res[base + t].astype(F32)
                ).astype(BF16)
            go(packed.at[core, pl.ds(base + 2 * (1 - value[b1]), 2)], self.in1.at[slot], b1)
        elif step == 1:
            for t in range(2):
                packed[core, two + t] = (
                    packed[core, two + t].astype(F32) + self.in1[slot, t].astype(F32)
                ).astype(BF16)
            go(packed.at[core, two + 1 - value[b2]], self.in2.at[slot], b2)
        elif step == 2:
            packed[core, one] = (
                packed[core, one].astype(F32) + self.in2[slot].astype(F32)
            ).astype(BF16)
            away = pl.ds(pl.multiple_of(half * (1 - value[b3]), 16), half)
            go(packed.at[core, one, away], self.in3.at[slot], b3)
        elif step < self.bits + 1:
            at = step - 3
            own = packed[core, one, rows] if at == 0 else self.in4[slot, 0, at - 1]
            came = self.in3[slot] if at == 0 else self.in4[slot, 1, at - 1]
            total = (own.astype(F32) + came.astype(F32)).astype(BF16)
            if step < self.bits:
                self.in4[slot, 0, at] = total
                go(self.in4.at[slot, 0, at], self.in4.at[slot, 1, at], step)
            else:
                res[one, rows] = total
                go(res.at[one, rows], res.at[one, rows], b3)
        elif step == self.bits + 1:
            go(res.at[one], res.at[one], b2)
        elif step == self.bits + 2:
            go(res.at[pl.ds(two, 2)], res.at[pl.ds(two, 2)], b1)


def layer_kernel(
    bits, buckets,
    lengths_ref, tokens_ref, cot_ref, wq_ref, wk_ref, wv_ref, wo_ref, wg_ref, wu_ref, wd_ref, ga_ref, gf_ref, table_ref,
    out_ref, dx_ref, res_ref, gain_out_ref,
    wqkv, wo, wg, wu, wd, gain_in, gain_own, gain, gain_sum, cs, bias,
    norm_one, norm_two, att, d_down, d_branch, qkv, probs, x_two, middle, hidden, d_up, d_gate,
    dn, d_att, d_qkv, packed, in1, in2, in3, in4, gain_buf,
    w_send, w_recv, w_local, half_send, half_recv, send_sem, recv_sem, gain_send, gain_recv,
):
    dp = lax.axis_index("dp")
    core = lax.axis_index("fsdp")
    total = buckets * BUCKET
    red = Reduction(
        bits, dp, core, packed, res_ref, (in1, in2, in3, in4), gain_buf,
        (half_send, half_recv, send_sem, recv_sem, gain_send, gain_recv),
    )
    barrier = pltpu.get_barrier_semaphore()
    for target in red.targets:
        pl.semaphore_signal(barrier, inc=1, device_id=target, device_id_type=MESH)

    scale = 1.0 / math.sqrt(HD)
    half = pl.ds(pl.multiple_of(core * TILE_ROWS, 16), TILE_ROWS)
    down_half = pl.ds(pl.multiple_of(core * (FF // 2), 128), FF // 2)
    wqkv[half, :] = jnp.concatenate(
        [
            (wq_ref[...].astype(F32) * scale).astype(BF16),
            wk_ref[...],
            wv_ref[...],
            jnp.zeros((TILE_ROWS, QKV - D - 2 * KVW), BF16),
        ],
        axis=1,
    )
    gain_own[0:1, :TILE_ROWS] = ga_ref[...].astype(F32).reshape(1, TILE_ROWS)
    gain_own[1:2, :TILE_ROWS] = gf_ref[...].astype(F32).reshape(1, TILE_ROWS)
    pl.semaphore_wait(barrier, len(red.targets))

    whole = [
        (wqkv.at[half], wqkv.at[half]), (wo_ref, wo.at[half]), (wg_ref, wg.at[half]),
        (wu_ref, wu.at[half]), (wd_ref, wd.at[:, down_half]), (gain_own, gain_in),
    ]
    arrivals, locals_ = [], []
    for i, (src, dst) in enumerate(whole):
        arrivals.append(red.start(remote(src, dst, w_send.at[i], w_recv.at[i], red.mate)))
        if 1 <= i <= 4:
            copy = pltpu.make_async_copy(src, dst, w_local.at[i - 1])
            copy.start()
            locals_.append(copy)

    def weight(i):
        if i >= 1:
            locals_[i - 1].wait()
        arrivals[i].wait_recv()

    def lanes(b):
        return slice(b * BUCKET, (b + 1) * BUCKET)

    place = lax.broadcasted_iota(jnp.int32, (BUCKET, BUCKET), 1)
    other = lax.broadcasted_iota(jnp.int32, (BUCKET, BUCKET), 0)
    alive = []
    for b in range(buckets):
        begin = jnp.zeros((BUCKET, BUCKET), jnp.int32)
        bound = 0
        for j in range(lengths_ref.shape[1]):
            bound = bound + lengths_ref[b, j]
            begin = begin + jnp.where(place >= bound, lengths_ref[b, j], 0)
        pick = jnp.where(place - begin == other, 1.0, 0.0).astype(BF16)
        parts = nn(table_ref[...], pick)
        cs[:, lanes(b)] = parts[:HD] + parts[HD : 2 * HD] + parts[2 * HD :]
        bias[b] = jnp.where((other >= begin) & (other <= place), 0.0, -1e30)
        alive.append((place[:1] < bound).astype(F32))

    d_qkv[D + 2 * KVW :, :] = jnp.zeros((QKV - D - 2 * KVW, 2 * total), BF16)
    gain_sum[...] = jnp.zeros_like(gain_sum)
    gain_buf[0, 0] = jnp.zeros(gain_buf.shape[2:], F32)
    arrivals[5].wait_recv()
    wide = lax.broadcasted_iota(jnp.int32, (8, 640), 1)
    low_half = jnp.where(core == 0, gain_own[...], gain_in[...])
    high_half = jnp.where(core == 0, gain_in[...], gain_own[...])
    gains = jnp.where(wide < TILE_ROWS, low_half, pltpu.roll(high_half, TILE_ROWS, 1))
    for i in range(2):
        gain[i] = jnp.broadcast_to(gains[i : i + 1, :D], (BUCKET, D)).T

    def x_of(p, b, rows=slice(None)):
        if p == 0:
            return tokens_ref[b, rows, :].astype(F32)
        return x_two[rows, lanes(b)]

    def middle_of(p, b, rows=slice(None)):
        return middle[p, rows, lanes(b)]

    def norm_forward(p, read, i, dst):
        for b in range(buckets):
            x = read(p, b)
            inv = lax.rsqrt(jnp.sum(x * x, axis=0, keepdims=True) * (1.0 / D) + 1e-05)
            dst[:, lanes(p * buckets + b)] = (x * inv * gain[i]).astype(BF16)

    def norm_backward(p, read, i, low_to):
        block = 64
        stats = []
        for b in range(buckets):
            squares = jnp.zeros((8, BUCKET), F32)
            dots = jnp.zeros((8, BUCKET), F32)
            for k in range(0, D, block):
                rows = slice(k, k + block)
                x = read(p, b, rows)
                d = dn[rows, lanes(b)] * gain[i, rows, :]
                squares = squares + jnp.sum((x * x).reshape(block // 8, 8, BUCKET), axis=0)
                dots = dots + jnp.sum((d * x).reshape(block // 8, 8, BUCKET), axis=0)
            inv = lax.rsqrt(jnp.sum(squares, axis=0, keepdims=True) * (1.0 / D) + 1e-05)
            mean = jnp.sum(dots, axis=0, keepdims=True) * inv * (1.0 / D)
            stats.append((inv, mean))
        for k in range(0, D, block):
            rows = slice(k, k + block)
            gain_term = gain_sum[i, rows, :]
            for b in range(buckets):
                inv, mean = stats[b]
                hat = read(p, b, rows) * inv
                d = dn[rows, lanes(b)]
                gain_term = gain_term + d * hat
                new = dx_ref[b, rows, :] + inv * (d * gain[i, rows, :] - hat * mean)
                dx_ref[b, rows, :] = new
                if low_to is not None:
                    low_to[rows, lanes(b)] = new.astype(BF16)
            gain_sum[i, rows, :] = gain_term

    def rope(z, b, sign):
        first, second = z[: HD // 2], z[HD // 2 :]
        cosines, sines = cs[: HD // 2, lanes(b)], cs[HD // 2 :, lanes(b)]
        if sign < 0:
            return jnp.concatenate([first * cosines + second * sines, second * cosines - first * sines], axis=0)
        return jnp.concatenate([first * cosines - second * sines, second * cosines + first * sines], axis=0)

    def head(h):
        return slice(HD * h, HD * (h + 1))

    def key_head(g):
        return head(HEADS + g)

    def value_head(g):
        return head(HEADS + KV_HEADS + g)

    def forward(p):
        at = slice(p * total, (p + 1) * total)
        norm_forward(p, x_of, 0, norm_one)
        if p == 0:
            weight(0)
        z = tn(wqkv[:, : D + 2 * KVW], norm_one[:, at])
        for h in range(HEADS + KV_HEADS):
            for b in range(buckets):
                qkv[head(h), lanes(p * buckets + b)] = rope(z[head(h), lanes(b)], b, 1).astype(BF16)
        qkv[D + KVW :, at] = z[D + KVW :].astype(BF16)
        for b in range(buckets):
            here = lanes(p * buckets + b)
            for h in range(HEADS):
                g, i = divmod(h, GROUP)
                scores = tn(qkv[key_head(g), here], qkv[head(h), here]) + bias[b]
                e = jnp.exp(scores - jnp.max(scores, axis=0, keepdims=True))
                low = (e * (1.0 / jnp.sum(e, axis=0, keepdims=True))).astype(BF16)
                probs[p * buckets + b, g, :, lanes(i)] = low
                att[head(h), here] = nn(qkv[value_head(g), here], low).astype(BF16)
        if p == 0:
            weight(1)
        mixed = tn(wo[...], att[:, at])
        for b in range(buckets):
            middle[p, :, lanes(b)] = x_of(p, b) + mixed[:, lanes(b)]
        norm_forward(p, middle_of, 1, norm_two)
        if p == 0:
            weight(2)
            weight(3)
        for c in range(0, FF, CHUNK):
            rows = slice(c, c + CHUNK)
            gate = tn(wg[:, rows], norm_two[:, at])
            up = tn(wu[:, rows], norm_two[:, at])
            s = 1.0 / (1.0 + jnp.exp(-gate))
            silu = gate * s
            hidden[rows, at] = (silu * up).astype(BF16)
            d_up[rows, at] = silu.astype(BF16)
            d_gate[rows, at] = (up * (s + silu * (1.0 - s))).astype(BF16)
        if p == 0:
            weight(4)
        result = middle[p] + nn(wd[...], hidden[:, at])
        if p == 0:
            x_two[...] = result
        else:
            for b in range(buckets):
                out_ref[b] = (result[:, lanes(b)] * alive[b]).astype(BF16)
                grad = cot_ref[b].astype(F32) * alive[b]
                dx_ref[b] = grad
                d_down[:, lanes(buckets + b)] = grad.astype(BF16)

    def put(first, block):
        low = block.astype(BF16)
        for h in range(2):
            for j in range(2):
                packed[h, first + j] = low[TILE_ROWS * h : TILE_ROWS * (h + 1), 128 * j : 128 * (j + 1)]

    def grad_down():
        per = FF // 2 // CHUNK
        for c in range(FF // CHUNK):
            low = nt(d_down[...], hidden[c * CHUNK : (c + 1) * CHUNK, :]).astype(BF16)
            for h in range(2):
                for j in range(2):
                    packed[c // per, 6 * h + 2 * (c % per) + j] = low[
                        TILE_ROWS * h : TILE_ROWS * (h + 1), 128 * j : 128 * (j + 1)
                    ]

    def grad_ffn(wave, d):
        for c in range(FF // CHUNK):
            put(wave * TILES + 2 * c, nt(norm_two[...], d[c * CHUNK : (c + 1) * CHUNK, :]))

    def backward(p):
        at = slice(p * total, (p + 1) * total)
        if p == 0:
            grad_down()
            red.exchange(0)
        for c in range(0, FF, CHUNK):
            rows = slice(c, c + CHUNK)
            d_hidden = tn(wd[:, rows], d_down[:, at])
            d_up[rows, at] = (d_hidden * d_up[rows, at].astype(F32)).astype(BF16)
            d_gate[rows, at] = (d_hidden * d_gate[rows, at].astype(F32)).astype(BF16)
        if p == 0:
            red.step(0, 0)
            grad_ffn(1, d_gate)
            red.exchange(1)
            red.step(0, 1)
            grad_ffn(2, d_up)
            red.exchange(2)
            red.step(1, 0)
            red.step(0, 2)
        dn[...] = nn(wg[...], d_gate[:, at]) + nn(wu[...], d_up[:, at])
        if p == 0:
            red.step(2, 0)
            red.step(1, 1)
            red.step(0, 3)
        norm_backward(p, middle_of, 1, d_branch.at[:, at])
        d_att[...] = nn(wo[...], d_branch[:, at]).astype(BF16)
        if p == 0:
            red.step(1, 2)
            red.step(0, 4)
        todo = [(b, g) for b in range(buckets) for g in range(KV_HEADS)]
        for first in range(0, len(todo), 6):
            part = todo[first : first + 6]

            def three(ref, g, where):
                return jnp.concatenate([ref[head(h), where] for h in range(GROUP * g, GROUP * (g + 1))], axis=1)

            d_probs = [
                tn(qkv[value_head(g), lanes(p * buckets + b)], three(d_att, g, lanes(b))) for b, g in part
            ]
            d_scores = []
            for (b, g), d in zip(part, d_probs):
                pr = probs[p * buckets + b, g].astype(F32)
                d_scores.append((pr * (d - jnp.sum(d * pr, axis=0, keepdims=True))).astype(BF16))
            for (b, g), ds in zip(part, d_scores):
                here = lanes(p * buckets + b)
                d_query = nn(qkv[key_head(g), here], ds)
                for i in range(GROUP):
                    d_qkv[head(GROUP * g + i), here] = rope(d_query[:, lanes(i)], b, -1).astype(BF16)
                d_qkv[key_head(g), here] = rope(nt(three(qkv, g, here), ds), b, -1).astype(BF16)
                d_qkv[value_head(g), here] = nt(
                    three(d_att, g, lanes(b)), probs[p * buckets + b, g]
                ).astype(BF16)
        if p == 0:
            red.step(2, 1)
            red.step(1, 3)
            red.step(0, 5)
        dn[...] = nn(wqkv[...], d_qkv[:, at])
        if p == 0:
            red.step(2, 2)
            red.step(1, 4)
            red.step(0, 6)
        norm_backward(p, x_of, 0, d_down.at[:, :total] if p == 1 else None)

    forward(0)
    forward(1)
    backward(1)
    backward(0)
    for i in range(2):
        gain_buf[0, 0, i : i + 1, :D] = jnp.sum(gain_sum[i].T, axis=0, keepdims=True)
    red.gain_start(0)

    column = lax.broadcasted_iota(jnp.int32, (1, CHUNK), 1)
    for c in range(3):
        block = nt(norm_one[...], d_qkv[c * CHUNK : (c + 1) * CHUNK, :])
        put(3 * TILES + 2 * c, block * jnp.where(column + c * CHUNK < D, scale, 1.0))
    block = nt(norm_one[...], d_qkv[3 * CHUNK :, :])
    rest = nt(att[...], d_branch[2 * CHUNK :, :])
    put(3 * TILES + 6, jnp.concatenate([block[:, : D + 2 * KVW - 3 * CHUNK], rest], axis=1))
    for c in range(2):
        put(3 * TILES + 8 + 2 * c, nt(att[...], d_branch[c * CHUNK : (c + 1) * CHUNK, :]))
    red.exchange(3)

    for diagonal in range(WAVES + red.last):
        if diagonal <= bits:
            red.gain_finish(diagonal)
            if diagonal < bits:
                red.gain_start(diagonal + 1)
        for w in range(WAVES):
            if 0 <= diagonal - w <= red.last:
                red.step(w, diagonal - w)
    sums = gain_buf[0, bits + 1]
    gain_out_ref[...] = jnp.where(core == 0, sums, pltpu.roll(sums, 640 - TILE_ROWS, 1))
    for copy in red.started:
        copy.wait_send()


def run_layer(bits, lengths, tokens, cotangent, weights, gains):
    buckets = tokens.shape[0]
    total = buckets * BUCKET
    slots = WAVES * STREAMS
    half = (TILE_ROWS // 2, 128)
    steps = bits + 3
    vmem = pl.BlockSpec(memory_space=pltpu.VMEM)
    hbm = pl.BlockSpec(memory_space=pl.ANY)
    dma = pltpu.SemaphoreType.DMA
    grads = (WAVES * TILES, TILE_ROWS, 128)
    scratch = [
        ((D, QKV), BF16), ((D, D), BF16), ((D, FF), BF16), ((D, FF), BF16), ((D, FF), BF16),
        ((8, 640), F32), ((8, 640), F32), ((2, D, BUCKET), F32), ((2, D, BUCKET), F32),
        ((HD, total), F32), ((buckets, BUCKET, BUCKET), F32),
        ((D, 2 * total), BF16), ((D, 2 * total), BF16), ((D, 2 * total), BF16),
        ((D, 2 * total), BF16), ((D, 2 * total), BF16),
        ((D + 2 * KVW, 2 * total), BF16),
        ((2 * buckets, KV_HEADS, BUCKET, GROUP * BUCKET), BF16),
        ((D, total), F32), ((2, D, total), F32),
        ((FF, 2 * total), BF16), ((FF, 2 * total), BF16), ((FF, 2 * total), BF16),
        ((D, total), F32), ((D, total), BF16), ((QKV, 2 * total), BF16),
        ((2, *grads), BF16), ((slots, 2, TILE_ROWS, 128), BF16), ((slots, TILE_ROWS, 128), BF16),
        ((slots, *half), BF16), ((slots, 2, bits - 3, *half), BF16), ((2, bits + 2, 8, 640), F32),
    ]
    return pl.pallas_call(
        functools.partial(layer_kernel, bits, buckets),
        out_shape=(
            jax.ShapeDtypeStruct((buckets, D, BUCKET), BF16),
            jax.ShapeDtypeStruct((buckets, D, BUCKET), F32),
            jax.ShapeDtypeStruct(grads, BF16),
            jax.ShapeDtypeStruct((8, 640), F32),
        ),
        in_specs=[pl.BlockSpec(memory_space=pltpu.SMEM)] + [vmem] * 5 + [hbm] * 4 + [vmem] * 3,
        out_specs=(vmem,) * 4,
        scratch_shapes=[pltpu.VMEM(shape, dtype) for shape, dtype in scratch]
        + [
            dma((6,)), dma((6,)), dma((4,)), dma((WAVES,)), dma((WAVES,)), dma((slots, steps)),
            dma((slots, steps)), dma((bits + 1,)), dma((bits + 1,)),
        ],
        compiler_params=pltpu.CompilerParams(
            collective_id=0, has_side_effects=True, vmem_limit_bytes=63 << 20
        ),
    )(lengths, tokens, cotangent, *weights, *gains, jnp.asarray(rope_table()))


def unpack_kernel(
    res_ref, out_in, dx_in, gain_in,
    out_ref, dx_ref, gq, gk, gv, go, gg, gu, gd, ga, gf,
):
    out_ref[...] = out_in[...]
    dx_ref[...] = dx_in[...]

    def tile(t):
        return res_ref[t].astype(F32)

    for j in range(6):
        for h in range(2):
            gd[TILE_ROWS * h : TILE_ROWS * (h + 1), 128 * j : 128 * (j + 1)] = tile(6 * h + j)
    for j in range(TILES):
        gg[:, 128 * j : 128 * (j + 1)] = tile(TILES + j)
        gu[:, 128 * j : 128 * (j + 1)] = tile(2 * TILES + j)
    first = 3 * TILES
    for j in range(4):
        gq[:, 128 * j : 128 * (j + 1)] = tile(first + j)
        go[:, 128 * j : 128 * (j + 1)] = tile(first + 8 + j)
    shared = tile(first + 4)
    gq[:, 512:] = shared[:, :64]
    key = tile(first + 5)
    gk[...] = jnp.concatenate([shared[:, 64:], key], axis=1)
    last = tile(first + 7)
    gv[...] = jnp.concatenate([tile(first + 6), last[:, :64]], axis=1)
    go[:, 512:] = last[:, 64:]
    ga[...] = gain_in[0, :TILE_ROWS]
    gf[...] = gain_in[1, :TILE_ROWS]


def unpack(res, output, input_grad, gain_sum):
    shapes = [
        (TILE_ROWS, D), (TILE_ROWS, KVW), (TILE_ROWS, KVW), (TILE_ROWS, D), (TILE_ROWS, FF), (TILE_ROWS, FF),
        (D, FF // 2), (TILE_ROWS,), (TILE_ROWS,),
    ]
    vmem = pl.BlockSpec(memory_space=pltpu.VMEM)
    return pl.pallas_call(
        unpack_kernel,
        out_shape=(
            jax.ShapeDtypeStruct(output.shape, output.dtype),
            jax.ShapeDtypeStruct(input_grad.shape, input_grad.dtype),
            *(jax.ShapeDtypeStruct(shape, F32) for shape in shapes),
        ),
        in_specs=[vmem] * 4,
        out_specs=(vmem,) * 11,
        compiler_params=pltpu.CompilerParams(vmem_limit_bytes=48 << 20),
    )(res, output, input_grad, gain_sum)


def on_device(
    bits, tokens, cotangent, lengths, w_query, w_key, w_value, w_out, w_gate, w_up, w_down, gain_attn, gain_ffn,
):
    output, input_grad, res, gain_sum = run_layer(
        bits,
        lengths[:, 0],
        tokens[:, 0].transpose(0, 2, 1),
        cotangent[:, 0].transpose(0, 2, 1),
        (w_query, w_key, w_value, w_out, w_gate, w_up, w_down.T),
        (gain_attn, gain_ffn),
    )
    output, input_grad, gq, gk, gv, go, gg, gu, gd, ga, gf = unpack(res, output, input_grad, gain_sum)
    return (
        output.transpose(0, 2, 1)[:, None], input_grad.transpose(0, 2, 1)[:, None],
        gq, gk, gv, go, gg, gu, gd.T, ga, gf,
    )


def solution(mesh):
    rows = P(None, ("dp", "fsdp"), None, None)
    weight = P("fsdp", None)
    in_specs = (rows, rows, P(None, ("dp", "fsdp"), None)) + (weight,) * 7 + (P("fsdp"),) * 2
    out_specs = (rows, rows) + (weight,) * 7 + (P("fsdp"),) * 2
    bits = mesh.shape["dp"].bit_length() - 1
    return jax.shard_map(
        functools.partial(on_device, bits),
        mesh=mesh,
        in_specs=in_specs,
        out_specs=out_specs,
        check_vma=False,
    )
```

```python
import functools
import math

import jax
import jax.numpy as jnp
import ml_dtypes
import numpy as np
from jax import lax
from jax.experimental import pallas as pl
from jax.experimental.pallas import tpu as pltpu
from jax.sharding import PartitionSpec as P

HEADS = 9
KV_HEADS = 3
GROUP = HEADS // KV_HEADS
HD = 64
D = 576
FF = 1536
KVW = KV_HEADS * HD
BUCKET = 128
MESH = pl.DeviceIdType.MESH
F32 = jnp.float32
BF16 = jnp.bfloat16

WAVES = 4
STREAMS = 3
TILES = 4 * STREAMS
TILE_ROWS = 288
QKV = 1024
CHUNK = 256
ATTEND = 6


def nn(a, b):
    return lax.dot_general(a, b, (((1,), (0,)), ((), ())), preferred_element_type=F32)


def nt(a, b):
    return lax.dot_general(a, b, (((1,), (1,)), ((), ())), preferred_element_type=F32)


def tn(a, b):
    return lax.dot_general(a, b, (((0,), (0,)), ((), ())), preferred_element_type=F32)


def rope_table():
    inverse = np.exp(np.arange(HD // 2) * (-2.0 * math.log(10000.0) / HD))
    angles = inverse[:, None] * np.arange(BUCKET)[None, :]
    rest = np.concatenate([np.cos(angles), np.sin(angles)], axis=0)
    parts = []
    for unused in range(3):
        part = rest.astype(ml_dtypes.bfloat16)
        parts.append(part)
        rest = rest - part.astype(np.float64)
    return np.concatenate(parts, axis=0)


def stream_bits(wave, stream):
    if stream == 0:
        return (0, 1, 2)
    if stream == 1:
        return (1, 0, 2)
    return (2, 0, 1) if wave % 2 == 0 else (2, 1, 0)


TILE_TIME, STEP_TIME, WAVE_TIME, WAVE_STEP_TIME = 1.61, 2.4, 1.6, 1.6
SLACK = 1.0
PARTS = (
    ("down", 2.1, 0), ("gated", 1.7, None), ("gate", 2.1, 1), ("up", 2.1, 2), ("ffn", 2.1, None),
    ("norm_two", 0.75, None), ("branch", 0.7, None), ("scores_a", 1.0, None), ("scores_b", 1.0, None),
    ("qkv", 0.85, None), ("norm_one", 0.75, None), ("rest", 2.4, 3),
)


def plan_steps(bits):
    last = bits + 3
    free = {"core": 0.0, 0: 0.0, 1: 0.0, 2: 0.0, "far": 0.0}
    came, following, plan, now = {}, {}, {}, 0.0

    def send(w, s, k):
        b1, b2, b3 = stream_bits(w, s)
        links = {0: (b1, 2), 1: (b2, 1), 2: (b3, 0.5), bits: (b3, 0.5), bits + 1: (b2, 1), bits + 2: (b1, 2)}
        link, tiles = links.get(k, ("far", 0.5))
        time = tiles * TILE_TIME
        if link == "far":
            begin = max(now, free[2])
            free[2] = begin + time
            free["far"] = max(begin, free["far"]) + 2 * time
            came[w, s, k] = free["far"] + STEP_TIME + 0.6
        else:
            free[link] = max(now, free[link]) + time
            came[w, s, k] = free[link] + STEP_TIME

    def earliest():
        waiting = [(came[w] if k == 0 else came[w, s, k - 1], w, s, k) for (w, s), k in following.items() if k <= last]
        return min(waiting, default=None)

    for name, time, wave in PARTS + (("end", 0.0, None),):
        now += time
        steps = plan[name] = []
        if wave is not None:
            free["core"] = max(now, free["core"]) + WAVE_TIME
            came[wave] = free["core"] + WAVE_STEP_TIME
            following.update({(wave, s): 0 for s in range(STREAMS)})
        event = earliest()
        while event is not None and (name == "end" or event[0] <= now + SLACK):
            arrival, w, s, k = event
            now = max(now, arrival) + 0.08
            if k < last:
                send(w, s, k)
            following[w, s] = k + 1
            steps.append((w, s, k))
            event = earliest()
    return plan


def remote(src, dst, send, recv, target):
    return pltpu.make_async_remote_copy(
        src_ref=src, dst_ref=dst, send_sem=send, recv_sem=recv, device_id=target,
        device_id_type=MESH,
    )


class Reduction:
    def __init__(self, bits, dp, core, packed, res, ins, gain_buf, sems):
        self.bits, self.core, self.packed, self.res = bits, core, packed, res
        self.in1, self.in2, self.in3, self.in4 = ins
        self.gain_buf = gain_buf
        (
            self.half_send, self.half_recv, self.send_sem, self.recv_sem, self.gain_send, self.gain_recv,
        ) = sems
        self.value = [(dp // (1 << b)) % 2 for b in range(bits)]
        self.partner = [dp + (1 << b) * (1 - 2 * self.value[b]) for b in range(bits)]
        self.mate = (dp, 1 - core)
        self.targets = [self.mate] + [(self.partner[b], core) for b in range(bits)]
        self.last = bits + 3
        self.started, self.flight, self.halves, self.gain_copies = [], {}, {}, []
        self.plan, self.whole, self.whole_gains, self.count = plan_steps(bits), set(), set(), 0

    def start(self, copy):
        copy.start()
        self.started.append(copy)
        return copy

    def exchange(self, w):
        tiles = pl.ds(w * TILES, TILES)
        self.halves[w] = remote(
            self.packed.at[1 - self.core, tiles], self.res.at[tiles],
            self.half_send.at[w], self.half_recv.at[w], self.mate,
        )
        self.halves[w].start()

    def gain_start(self, i):
        target = self.targets[i]
        self.gain_copies.append(
            self.start(
                remote(
                    self.gain_buf.at[0, i], self.gain_buf.at[1, i], self.gain_send.at[i],
                    self.gain_recv.at[i], target,
                )
            )
        )

    def gain_finish(self, i):
        self.gain_copies[i].wait_recv()
        self.gain_buf[0, i + 1] = self.gain_buf[0, i] + self.gain_buf[1, i]

    def after(self, name):
        for part, unused, wave in PARTS:
            if part == name and wave is not None:
                self.exchange(wave)
        for w, s, step in self.plan[name]:
            if step == 0 and w not in self.whole:
                self.whole.add(w)
                self.halves[w].wait()
            self.stream_step(w, s, step)
            self.count += 1
            if name == "end" and self.count % 8 == 0:
                self.gain_step()

    def gain_step(self):
        i = len(self.gain_copies)
        if i > 0 and i not in self.whole_gains:
            self.gain_finish(i - 1)
            self.whole_gains.add(i)
        if i <= self.bits:
            self.gain_start(i)

    def stream_step(self, w, s, step):
        value, core, packed, res = self.value, self.core, self.packed, self.res
        b1, b2, b3 = stream_bits(w, s)
        base = w * TILES + 4 * s
        two = base + 2 * value[b1]
        one = two + value[b2]
        half = TILE_ROWS // 2
        rows = pl.ds(pl.multiple_of(half * value[b3], 16), half)
        slot = w * STREAMS + s

        def go(src, dst, bit):
            self.flight[(slot, step)] = self.start(
                remote(
                    src, dst, self.send_sem.at[slot, step], self.recv_sem.at[slot, step],
                    (self.partner[bit], core),
                )
            )

        if step > 0:
            self.flight[(slot, step - 1)].wait_recv()
        if step == 0:
            for t in range(4):
                packed[core, base + t] = (
                    packed[core, base + t].astype(F32) + res[base + t].astype(F32)
                ).astype(BF16)
            go(packed.at[core, pl.ds(base + 2 * (1 - value[b1]), 2)], self.in1.at[slot], b1)
        elif step == 1:
            for t in range(2):
                packed[core, two + t] = (
                    packed[core, two + t].astype(F32) + self.in1[slot, t].astype(F32)
                ).astype(BF16)
            go(packed.at[core, two + 1 - value[b2]], self.in2.at[slot], b2)
        elif step == 2:
            packed[core, one] = (
                packed[core, one].astype(F32) + self.in2[slot].astype(F32)
            ).astype(BF16)
            away = pl.ds(pl.multiple_of(half * (1 - value[b3]), 16), half)
            go(packed.at[core, one, away], self.in3.at[slot], b3)
        elif step < self.bits + 1:
            at = step - 3
            own = packed[core, one, rows] if at == 0 else self.in4[slot, 0, at - 1]
            came = self.in3[slot] if at == 0 else self.in4[slot, 1, at - 1]
            total = (own.astype(F32) + came.astype(F32)).astype(BF16)
            if step < self.bits:
                self.in4[slot, 0, at] = total
                go(self.in4.at[slot, 0, at], self.in4.at[slot, 1, at], step)
            else:
                res[one, rows] = total
                go(res.at[one, rows], res.at[one, rows], b3)
        elif step == self.bits + 1:
            go(res.at[one], res.at[one], b2)
        elif step == self.bits + 2:
            go(res.at[pl.ds(two, 2)], res.at[pl.ds(two, 2)], b1)


def layer_kernel(
    bits, buckets,
    lengths_ref, tokens_ref, cot_ref, wq_ref, wk_ref, wv_ref, wo_ref, wg_ref, wu_ref, wd_ref, ga_ref, gf_ref, table_ref,
    out_ref, dx_ref, res_ref, gain_out_ref,
    wqkv, wo, wg, wu, wd, gain_in, gain_own, gain, gain_sum, cs, bias,
    norm_one, norm_two, att, d_down, d_branch, qkv, probs, x_two, middle, hidden, d_up, d_gate,
    dn, d_att, d_qkv, packed, in1, in2, in3, in4, gain_buf,
    w_send, w_recv, w_local, half_send, half_recv, send_sem, recv_sem, gain_send, gain_recv,
):
    dp = lax.axis_index("dp")
    core = lax.axis_index("fsdp")
    total = buckets * BUCKET
    red = Reduction(
        bits, dp, core, packed, res_ref, (in1, in2, in3, in4), gain_buf,
        (half_send, half_recv, send_sem, recv_sem, gain_send, gain_recv),
    )
    barrier = pltpu.get_barrier_semaphore()
    for target in red.targets:
        pl.semaphore_signal(barrier, inc=1, device_id=target, device_id_type=MESH)

    scale = 1.0 / math.sqrt(HD)
    half = pl.ds(pl.multiple_of(core * TILE_ROWS, 16), TILE_ROWS)
    down_half = pl.ds(pl.multiple_of(core * (FF // 2), 128), FF // 2)
    wqkv[half, :] = jnp.concatenate(
        [
            (wq_ref[...].astype(F32) * scale).astype(BF16),
            wk_ref[...],
            wv_ref[...],
            jnp.zeros((TILE_ROWS, QKV - D - 2 * KVW), BF16),
        ],
        axis=1,
    )
    gain_own[0:1, :TILE_ROWS] = ga_ref[...].astype(F32).reshape(1, TILE_ROWS)
    gain_own[1:2, :TILE_ROWS] = gf_ref[...].astype(F32).reshape(1, TILE_ROWS)
    pl.semaphore_wait(barrier, len(red.targets))

    whole = [
        (wqkv.at[half], wqkv.at[half]), (wo_ref, wo.at[half]), (wg_ref, wg.at[half]),
        (wu_ref, wu.at[half]), (wd_ref, wd.at[:, down_half]), (gain_own, gain_in),
    ]
    arrivals, locals_ = {}, []
    for i in (5, 0, 1, 2, 3, 4):
        src, dst = whole[i]
        arrivals[i] = red.start(remote(src, dst, w_send.at[i], w_recv.at[i], red.mate))
        if 1 <= i <= 4:
            copy = pltpu.make_async_copy(src, dst, w_local.at[i - 1])
            copy.start()
            locals_.append(copy)

    def weight(i):
        if i >= 1:
            locals_[i - 1].wait()
        arrivals[i].wait_recv()

    def lanes(b):
        return slice(b * BUCKET, (b + 1) * BUCKET)

    place = lax.broadcasted_iota(jnp.int32, (BUCKET, BUCKET), 1)
    other = lax.broadcasted_iota(jnp.int32, (BUCKET, BUCKET), 0)
    alive = []
    for b in range(buckets):
        begin = jnp.zeros((BUCKET, BUCKET), jnp.int32)
        bound = 0
        for j in range(lengths_ref.shape[1]):
            bound = bound + lengths_ref[b, j]
            begin = begin + jnp.where(place >= bound, lengths_ref[b, j], 0)
        pick = jnp.where(place - begin == other, 1.0, 0.0).astype(BF16)
        parts = nn(table_ref[...], pick)
        cs[:, lanes(b)] = parts[:HD] + parts[HD : 2 * HD] + parts[2 * HD :]
        bias[b] = jnp.where((other >= begin) & (other <= place), 0.0, -1e30)
        alive.append((place[:1] < bound).astype(F32))

    d_qkv[D + 2 * KVW :, :] = jnp.zeros((QKV - D - 2 * KVW, 2 * total), BF16)
    gain_sum[...] = jnp.zeros_like(gain_sum)
    gain_buf[0, 0] = jnp.zeros(gain_buf.shape[2:], F32)
    arrivals[5].wait_recv()
    wide = lax.broadcasted_iota(jnp.int32, (8, 640), 1)
    low_half = jnp.where(core == 0, gain_own[...], gain_in[...])
    high_half = jnp.where(core == 0, gain_in[...], gain_own[...])
    gains = jnp.where(wide < TILE_ROWS, low_half, pltpu.roll(high_half, TILE_ROWS, 1))
    for i in range(2):
        gain[i] = jnp.broadcast_to(gains[i : i + 1, :D], (BUCKET, D)).T

    def x_of(p, b, rows=slice(None)):
        if p == 0:
            return tokens_ref[b, rows, :].astype(F32)
        return x_two[rows, lanes(b)]

    def middle_of(p, b, rows=slice(None)):
        return middle[p, rows, lanes(b)]

    def norm_forward(p, read, i, dst):
        for b in range(buckets):
            x = read(p, b)
            inv = lax.rsqrt(jnp.sum(x * x, axis=0, keepdims=True) * (1.0 / D) + 1e-05)
            dst[:, lanes(p * buckets + b)] = (x * inv * gain[i]).astype(BF16)

    def norm_backward(p, read, i, low_to):
        block = 64
        stats = []
        for b in range(buckets):
            squares = jnp.zeros((8, BUCKET), F32)
            dots = jnp.zeros((8, BUCKET), F32)
            for k in range(0, D, block):
                rows = slice(k, k + block)
                x = read(p, b, rows)
                d = dn[rows, lanes(b)] * gain[i, rows, :]
                squares = squares + jnp.sum((x * x).reshape(block // 8, 8, BUCKET), axis=0)
                dots = dots + jnp.sum((d * x).reshape(block // 8, 8, BUCKET), axis=0)
            inv = lax.rsqrt(jnp.sum(squares, axis=0, keepdims=True) * (1.0 / D) + 1e-05)
            mean = jnp.sum(dots, axis=0, keepdims=True) * inv * (1.0 / D)
            stats.append((inv, mean))
        for k in range(0, D, block):
            rows = slice(k, k + block)
            gain_term = gain_sum[i, rows, :]
            for b in range(buckets):
                inv, mean = stats[b]
                hat = read(p, b, rows) * inv
                d = dn[rows, lanes(b)]
                gain_term = gain_term + d * hat
                new = dx_ref[b, rows, :] + inv * (d * gain[i, rows, :] - hat * mean)
                dx_ref[b, rows, :] = new
                if low_to is not None:
                    low_to[rows, lanes(b)] = new.astype(BF16)
            gain_sum[i, rows, :] = gain_term

    def rope(z, b, sign):
        first, second = z[: HD // 2], z[HD // 2 :]
        cosines, sines = cs[: HD // 2, lanes(b)], cs[HD // 2 :, lanes(b)]
        if sign < 0:
            return jnp.concatenate([first * cosines + second * sines, second * cosines - first * sines], axis=0)
        return jnp.concatenate([first * cosines - second * sines, second * cosines + first * sines], axis=0)

    def head(h):
        return slice(HD * h, HD * (h + 1))

    def key_head(g):
        return head(HEADS + g)

    def value_head(g):
        return head(HEADS + KV_HEADS + g)

    def three(ref, g, where):
        return jnp.concatenate([ref[head(h), where] for h in range(GROUP * g, GROUP * (g + 1))], axis=1)

    def forward(p):
        at = slice(p * total, (p + 1) * total)
        norm_forward(p, x_of, 0, norm_one)
        if p == 0:
            weight(0)
        z = tn(wqkv[:, : D + 2 * KVW], norm_one[:, at])
        for h in range(HEADS + KV_HEADS):
            for b in range(buckets):
                qkv[head(h), lanes(p * buckets + b)] = rope(z[head(h), lanes(b)], b, 1).astype(BF16)
        qkv[D + KVW :, at] = z[D + KVW :].astype(BF16)
        todo = [(b, g) for b in range(buckets) for g in range(KV_HEADS)]
        for first in range(0, len(todo), ATTEND):
            part = [(b, g, lanes(p * buckets + b)) for b, g in todo[first : first + ATTEND]]
            scores = [
                tn(qkv[key_head(g), here], three(qkv, g, here)) + jnp.concatenate([bias[b]] * GROUP, axis=1)
                for b, g, here in part
            ]
            lows = []
            for (b, g, here), score in zip(part, scores):
                e = jnp.exp(score - jnp.max(score, axis=0, keepdims=True))
                low = (e * (1.0 / jnp.sum(e, axis=0, keepdims=True))).astype(BF16)
                probs[p * buckets + b, g] = low
                lows.append(low)
            for (b, g, here), low in zip(part, lows):
                mixed = nn(qkv[value_head(g), here], low).astype(BF16)
                for i in range(GROUP):
                    att[head(GROUP * g + i), here] = mixed[:, lanes(i)]
        if p == 0:
            weight(1)
        mixed = tn(wo[...], att[:, at])
        for b in range(buckets):
            middle[p, :, lanes(b)] = x_of(p, b) + mixed[:, lanes(b)]
        norm_forward(p, middle_of, 1, norm_two)
        if p == 0:
            weight(2)
            weight(3)
        for c in range(0, FF, CHUNK):
            rows = slice(c, c + CHUNK)
            gate = tn(wg[:, rows], norm_two[:, at])
            up = tn(wu[:, rows], norm_two[:, at])
            s = 1.0 / (1.0 + jnp.exp(-gate))
            silu = gate * s
            hidden[rows, at] = (silu * up).astype(BF16)
            d_up[rows, at] = silu.astype(BF16)
            d_gate[rows, at] = (up * (s + silu * (1.0 - s))).astype(BF16)
        if p == 0:
            weight(4)
        result = middle[p] + nn(wd[...], hidden[:, at])
        if p == 0:
            x_two[...] = result
        else:
            for b in range(buckets):
                out_ref[b] = (result[:, lanes(b)] * alive[b]).astype(BF16)
                grad = cot_ref[b].astype(F32) * alive[b]
                dx_ref[b] = grad
                d_down[:, lanes(buckets + b)] = grad.astype(BF16)

    def put(first, block):
        low = block.astype(BF16)
        for h in range(2):
            for j in range(2):
                packed[h, first + j] = low[TILE_ROWS * h : TILE_ROWS * (h + 1), 128 * j : 128 * (j + 1)]

    def grad_down():
        per = FF // 2 // CHUNK
        for c in range(FF // CHUNK):
            low = nt(d_down[...], hidden[c * CHUNK : (c + 1) * CHUNK, :]).astype(BF16)
            for h in range(2):
                for j in range(2):
                    packed[c // per, 6 * h + 2 * (c % per) + j] = low[
                        TILE_ROWS * h : TILE_ROWS * (h + 1), 128 * j : 128 * (j + 1)
                    ]

    def grad_ffn(wave, d):
        for c in range(FF // CHUNK):
            put(wave * TILES + 2 * c, nt(norm_two[...], d[c * CHUNK : (c + 1) * CHUNK, :]))

    def backward(p):
        at = slice(p * total, (p + 1) * total)
        if p == 0:
            grad_down()
            red.after("down")
        for c in range(0, FF, CHUNK):
            rows = slice(c, c + CHUNK)
            d_hidden = tn(wd[:, rows], d_down[:, at])
            d_up[rows, at] = (d_hidden * d_up[rows, at].astype(F32)).astype(BF16)
            d_gate[rows, at] = (d_hidden * d_gate[rows, at].astype(F32)).astype(BF16)
        if p == 0:
            red.after("gated")
            grad_ffn(1, d_gate)
            red.after("gate")
            grad_ffn(2, d_up)
            red.after("up")
        dn[...] = nn(wg[...], d_gate[:, at]) + nn(wu[...], d_up[:, at])
        if p == 0:
            red.after("ffn")
        norm_backward(p, middle_of, 1, d_branch.at[:, at])
        if p == 0:
            red.after("norm_two")
        d_att[...] = nn(wo[...], d_branch[:, at]).astype(BF16)
        if p == 0:
            red.after("branch")
        todo = [(b, g) for b in range(buckets) for g in range(KV_HEADS)]
        for first in range(0, len(todo), ATTEND):
            part = todo[first : first + ATTEND]
            d_probs = [
                tn(qkv[value_head(g), lanes(p * buckets + b)], three(d_att, g, lanes(b))) for b, g in part
            ]
            d_scores = []
            for (b, g), d in zip(part, d_probs):
                pr = probs[p * buckets + b, g].astype(F32)
                d_scores.append((pr * (d - jnp.sum(d * pr, axis=0, keepdims=True))).astype(BF16))
            for (b, g), ds in zip(part, d_scores):
                here = lanes(p * buckets + b)
                d_query = nn(qkv[key_head(g), here], ds)
                for i in range(GROUP):
                    d_qkv[head(GROUP * g + i), here] = rope(d_query[:, lanes(i)], b, -1).astype(BF16)
                d_qkv[key_head(g), here] = rope(nt(three(qkv, g, here), ds), b, -1).astype(BF16)
                d_qkv[value_head(g), here] = nt(
                    three(d_att, g, lanes(b)), probs[p * buckets + b, g]
                ).astype(BF16)
            if p == 0:
                red.after("scores_a" if first == 0 else "scores_b")
        dn[...] = nn(wqkv[...], d_qkv[:, at])
        if p == 0:
            red.after("qkv")
        norm_backward(p, x_of, 0, d_down.at[:, :total] if p == 1 else None)
        if p == 0:
            red.after("norm_one")

    forward(0)
    forward(1)
    backward(1)
    backward(0)
    for i in range(2):
        gain_buf[0, 0, i : i + 1, :D] = jnp.sum(gain_sum[i].T, axis=0, keepdims=True)
    red.gain_step()

    column = lax.broadcasted_iota(jnp.int32, (1, CHUNK), 1)
    for c in range(3):
        block = nt(norm_one[...], d_qkv[c * CHUNK : (c + 1) * CHUNK, :])
        put(3 * TILES + 2 * c, block * jnp.where(column + c * CHUNK < D, scale, 1.0))
    block = nt(norm_one[...], d_qkv[3 * CHUNK :, :])
    rest = nt(att[...], d_branch[2 * CHUNK :, :])
    put(3 * TILES + 6, jnp.concatenate([block[:, : D + 2 * KVW - 3 * CHUNK], rest], axis=1))
    for c in range(2):
        put(3 * TILES + 8 + 2 * c, nt(att[...], d_branch[c * CHUNK : (c + 1) * CHUNK, :]))
    red.after("rest")
    red.after("end")
    while len(red.whole_gains) <= bits:
        red.gain_step()
    sums = gain_buf[0, bits + 1]
    gain_out_ref[...] = jnp.where(core == 0, sums, pltpu.roll(sums, 640 - TILE_ROWS, 1))
    for copy in red.started:
        copy.wait_send()


def run_layer(bits, lengths, tokens, cotangent, weights, gains):
    buckets = tokens.shape[0]
    total = buckets * BUCKET
    slots = WAVES * STREAMS
    half = (TILE_ROWS // 2, 128)
    steps = bits + 3
    vmem = pl.BlockSpec(memory_space=pltpu.VMEM)
    hbm = pl.BlockSpec(memory_space=pl.ANY)
    dma = pltpu.SemaphoreType.DMA
    grads = (WAVES * TILES, TILE_ROWS, 128)
    scratch = [
        ((D, QKV), BF16), ((D, D), BF16), ((D, FF), BF16), ((D, FF), BF16), ((D, FF), BF16),
        ((8, 640), F32), ((8, 640), F32), ((2, D, BUCKET), F32), ((2, D, BUCKET), F32),
        ((HD, total), F32), ((buckets, BUCKET, BUCKET), F32),
        ((D, 2 * total), BF16), ((D, 2 * total), BF16), ((D, 2 * total), BF16),
        ((D, 2 * total), BF16), ((D, 2 * total), BF16),
        ((D + 2 * KVW, 2 * total), BF16),
        ((2 * buckets, KV_HEADS, BUCKET, GROUP * BUCKET), BF16),
        ((D, total), F32), ((2, D, total), F32),
        ((FF, 2 * total), BF16), ((FF, 2 * total), BF16), ((FF, 2 * total), BF16),
        ((D, total), F32), ((D, total), BF16), ((QKV, 2 * total), BF16),
        ((2, *grads), BF16), ((slots, 2, TILE_ROWS, 128), BF16), ((slots, TILE_ROWS, 128), BF16),
        ((slots, *half), BF16), ((slots, 2, bits - 3, *half), BF16), ((2, bits + 2, 8, 640), F32),
    ]
    return pl.pallas_call(
        functools.partial(layer_kernel, bits, buckets),
        out_shape=(
            jax.ShapeDtypeStruct((buckets, D, BUCKET), BF16),
            jax.ShapeDtypeStruct((buckets, D, BUCKET), F32),
            jax.ShapeDtypeStruct(grads, BF16),
            jax.ShapeDtypeStruct((8, 640), F32),
        ),
        in_specs=[pl.BlockSpec(memory_space=pltpu.SMEM)] + [vmem] * 5 + [hbm] * 4 + [vmem] * 3,
        out_specs=(vmem,) * 4,
        scratch_shapes=[pltpu.VMEM(shape, dtype) for shape, dtype in scratch]
        + [
            dma((6,)), dma((6,)), dma((4,)), dma((WAVES,)), dma((WAVES,)), dma((slots, steps)),
            dma((slots, steps)), dma((bits + 1,)), dma((bits + 1,)),
        ],
        compiler_params=pltpu.CompilerParams(
            collective_id=0, has_side_effects=True, vmem_limit_bytes=63 << 20
        ),
    )(lengths, tokens, cotangent, *weights, *gains, jnp.asarray(rope_table()))


def unpack_kernel(
    res_hbm, out_in, dx_in, gain_in,
    out_ref, dx_ref, gq, gk, gv, go, gg, gu, gd, ga, gf,
    res_ref, out_block, dx_block, query, key, value, branch, gate, up, down, in_sem, out_sem,
):
    arrivals = [
        pltpu.make_async_copy(res_hbm.at[pl.ds(w * TILES, TILES)], res_ref.at[pl.ds(w * TILES, TILES)], in_sem.at[w])
        for w in range(WAVES)
    ]
    arrivals.append(pltpu.make_async_copy(dx_in, dx_block, in_sem.at[WAVES]))
    arrivals.append(pltpu.make_async_copy(out_in, out_block, in_sem.at[WAVES + 1]))
    for copy in arrivals:
        copy.start()
    copies = []
    ga[...] = gain_in[0, :TILE_ROWS]
    gf[...] = gain_in[1, :TILE_ROWS]

    def tile(t):
        return res_ref[t].astype(F32)

    def leave(src, dst):
        copy = pltpu.make_async_copy(src, dst, out_sem.at[len(copies)])
        copy.start()
        copies.append(copy)

    arrivals[0].wait()
    for j in range(6):
        for h in range(2):
            down[TILE_ROWS * h : TILE_ROWS * (h + 1), 128 * j : 128 * (j + 1)] = tile(6 * h + j)
    leave(down, gd)
    for w, block, dst in ((1, gate, gg), (2, up, gu)):
        arrivals[w].wait()
        for j in range(TILES):
            block[:, 128 * j : 128 * (j + 1)] = tile(w * TILES + j)
        leave(block, dst)
    arrivals[3].wait()
    first = 3 * TILES
    for j in range(4):
        query[:, 128 * j : 128 * (j + 1)] = tile(first + j)
        branch[:, 128 * j : 128 * (j + 1)] = tile(first + 8 + j)
    shared, last = tile(first + 4), tile(first + 7)
    query[:, 512:] = shared[:, :64]
    leave(query, gq)
    branch[:, 512:] = last[:, 64:]
    leave(branch, go)
    key[...] = jnp.concatenate([shared[:, 64:], tile(first + 5)], axis=1)
    leave(key, gk)
    value[...] = jnp.concatenate([tile(first + 6), last[:, :64]], axis=1)
    leave(value, gv)
    arrivals[WAVES].wait()
    leave(dx_block, dx_ref)
    arrivals[WAVES + 1].wait()
    leave(out_block, out_ref)
    for copy in copies:
        copy.wait()


def unpack(res, output, input_grad, gain_sum):
    shapes = [
        (TILE_ROWS, D), (TILE_ROWS, KVW), (TILE_ROWS, KVW), (TILE_ROWS, D), (TILE_ROWS, FF), (TILE_ROWS, FF),
        (D, FF // 2),
    ]
    vmem = pl.BlockSpec(memory_space=pltpu.VMEM)
    hbm = pl.BlockSpec(memory_space=pl.ANY)
    dma = pltpu.SemaphoreType.DMA
    return pl.pallas_call(
        unpack_kernel,
        out_shape=(
            jax.ShapeDtypeStruct(output.shape, output.dtype),
            jax.ShapeDtypeStruct(input_grad.shape, input_grad.dtype),
            *(jax.ShapeDtypeStruct(shape, F32) for shape in shapes + [(TILE_ROWS,)] * 2),
        ),
        in_specs=[hbm] * 3 + [vmem],
        out_specs=(hbm,) * 9 + (vmem,) * 2,
        scratch_shapes=[pltpu.VMEM(a.shape, a.dtype) for a in (res, output, input_grad)]
        + [pltpu.VMEM(shape, F32) for shape in shapes]
        + [dma((WAVES + 2,)), dma((len(shapes) + 2,))],
        compiler_params=pltpu.CompilerParams(vmem_limit_bytes=63 << 20),
    )(res, output, input_grad, gain_sum)


def on_device(
    bits, tokens, cotangent, lengths, w_query, w_key, w_value, w_out, w_gate, w_up, w_down, gain_attn, gain_ffn,
):
    output, input_grad, res, gain_sum = run_layer(
        bits,
        lengths[:, 0],
        tokens[:, 0].transpose(0, 2, 1),
        cotangent[:, 0].transpose(0, 2, 1),
        (w_query, w_key, w_value, w_out, w_gate, w_up, w_down.T),
        (gain_attn, gain_ffn),
    )
    output, input_grad, gq, gk, gv, go, gg, gu, gd, ga, gf = unpack(res, output, input_grad, gain_sum)
    return (
        output.transpose(0, 2, 1)[:, None], input_grad.transpose(0, 2, 1)[:, None],
        gq, gk, gv, go, gg, gu, gd.T, ga, gf,
    )


def solution(mesh):
    rows = P(None, ("dp", "fsdp"), None, None)
    weight = P("fsdp", None)
    in_specs = (rows, rows, P(None, ("dp", "fsdp"), None)) + (weight,) * 7 + (P("fsdp"),) * 2
    out_specs = (rows, rows) + (weight,) * 7 + (P("fsdp"),) * 2
    bits = mesh.shape["dp"].bit_length() - 1
    return jax.shard_map(
        functools.partial(on_device, bits),
        mesh=mesh,
        in_specs=in_specs,
        out_specs=out_specs,
        check_vma=False,
    )
```

```python
import functools
import math

import jax
import jax.numpy as jnp
import ml_dtypes
import numpy as np
from jax import lax
from jax.experimental import pallas as pl
from jax.experimental.pallas import tpu as pltpu
from jax.sharding import PartitionSpec as P

HEADS = 9
KV_HEADS = 3
GROUP = HEADS // KV_HEADS
HD = 64
D = 576
FF = 1536
KVW = KV_HEADS * HD
BUCKET = 128
MESH = pl.DeviceIdType.MESH
F32 = jnp.float32
BF16 = jnp.bfloat16

WAVES = 4
STREAMS = 3
TILES = 4 * STREAMS
TILE_ROWS = 288
QKV = 1024
CHUNK = 256
ATTEND = 6


def nn(a, b):
    return lax.dot_general(a, b, (((1,), (0,)), ((), ())), preferred_element_type=F32)


def nt(a, b):
    return lax.dot_general(a, b, (((1,), (1,)), ((), ())), preferred_element_type=F32)


def tn(a, b):
    return lax.dot_general(a, b, (((0,), (0,)), ((), ())), preferred_element_type=F32)


def rope_table():
    inverse = np.exp(np.arange(HD // 2) * (-2.0 * math.log(10000.0) / HD))
    angles = inverse[:, None] * np.arange(BUCKET)[None, :]
    rest = np.concatenate([np.cos(angles), np.sin(angles)], axis=0)
    parts = []
    for unused in range(3):
        part = rest.astype(ml_dtypes.bfloat16)
        parts.append(part)
        rest = rest - part.astype(np.float64)
    return np.concatenate(parts, axis=0)


STREAM_BITS = (
    ((1, 2, 0), (0, 1, 2), (2, 1, 0)),
    ((1, 0, 2), (0, 2, 1), (2, 1, 0)),
    ((0, 2, 1), (1, 0, 2), (2, 1, 0)),
    ((2, 1, 0), (1, 0, 2), (0, 2, 1)),
)


def stream_bits(wave, stream):
    return STREAM_BITS[wave][stream]


TILE_TIME, STEP_TIME, WAVE_TIME, WAVE_STEP_TIME = 1.42, 2.65, 1.3, 1.5
STEP_RANK, WAVE_RANK, THIRD_RANK = 6.404041155859943, 5.683458090508361, 0.024984608445357243
PARTS = (
    ("down_a", 1.05, 0, 1.0), ("down_b", 1.05, None, 1.0), ("gated", 1.7, None, -1.0), ("gate_a", 1.05, None, -5.0),
    ("gate_b", 1.05, 1, 0.0), ("up_a", 1.05, None, 1.0), ("up_b", 1.05, 2, 0.3), ("ffn", 2.1, None, 0.6),
    ("norm_two", 0.75, None, -1.0), ("branch", 0.7, None, -5.0), ("scores_a", 1.0, None, 0.3),
    ("scores_b", 1.0, None, 0.0), ("rest", 2.1, 3, 0.6), ("qkv", 0.85, None, 0.6), ("norm_one", 1.1, None, -1.0),
    ("end", 0.0, None, 1e9),
)


def plan_steps(bits):
    last = bits + 3
    free = {"core": 0.0, 0: 0.0, 1: 0.0, 2: 0.0, "far": 0.0}
    waiting, plan, now = {}, {}, 0.0

    def sent(w, s, k):
        b1, b2, b3 = stream_bits(w, s)
        links = {0: (b1, 2), 1: (b2, 1), 2: (b3, 0.5), bits: (b3, 0.5), bits + 1: (b2, 1), bits + 2: (b1, 2)}
        link, tiles = links.get(k, ("far", 0.5))
        time = tiles * TILE_TIME
        if link == "far":
            begin = max(now, free[2])
            free[2] = begin + time
            free["far"] = max(begin, free["far"]) + 2 * time
            return free["far"] + STEP_TIME + 0.6
        free[link] = max(now, free[link]) + time
        return free[link] + STEP_TIME

    for name, time, wave, slack in PARTS:
        now += time
        limit = now + slack
        steps = plan[name] = []
        if wave is not None:
            free["core"] = max(now, free["core"]) + WAVE_TIME
            waiting.update({(wave, s): (free["core"] + WAVE_STEP_TIME, 0) for s in range(STREAMS)})
        while True:
            ranked = [
                (max(came, now) + STEP_RANK * k + WAVE_RANK * w + THIRD_RANK * (s == 2), came, w, s, k)
                for (w, s), (came, k) in waiting.items()
                if came <= limit
            ]
            if not ranked:
                break
            unused, came, w, s, k = min(ranked)
            now = max(now, came) + 0.2
            steps.append((w, s, k))
            if k < last:
                waiting[w, s] = (sent(w, s, k), k + 1)
            else:
                del waiting[w, s]
    return plan


def remote(src, dst, send, recv, target):
    return pltpu.make_async_remote_copy(
        src_ref=src, dst_ref=dst, send_sem=send, recv_sem=recv, device_id=target,
        device_id_type=MESH,
    )


class Reduction:
    def __init__(self, bits, dp, core, packed, res, res_out, ins, gain_buf, sems):
        self.bits, self.core, self.packed, self.res, self.res_out = bits, core, packed, res, res_out
        self.in1, self.in2, self.in3, self.in4 = ins
        self.gain_buf = gain_buf
        (
            self.half_send, self.half_recv, self.send_sem, self.recv_sem, self.gain_send, self.gain_recv, self.res_sem,
        ) = sems
        self.value = [(dp // (1 << b)) % 2 for b in range(bits)]
        self.partner = [dp + (1 << b) * (1 - 2 * self.value[b]) for b in range(bits)]
        self.mate = (dp, 1 - core)
        self.targets = [self.mate] + [(self.partner[b], core) for b in range(bits)]
        self.last = bits + 3
        self.started, self.flight, self.halves, self.gain_copies, self.leaving = [], {}, {}, [], []
        self.plan, self.whole, self.whole_gains, self.count = plan_steps(bits), set(), set(), 0

    def start(self, copy):
        copy.start()
        self.started.append(copy)
        return copy

    def exchange(self, w):
        tiles = pl.ds(w * TILES, TILES)
        self.halves[w] = remote(
            self.packed.at[1 - self.core, tiles], self.res.at[tiles],
            self.half_send.at[w], self.half_recv.at[w], self.mate,
        )
        self.halves[w].start()

    def gain_start(self, i):
        target = self.targets[i]
        self.gain_copies.append(
            self.start(
                remote(
                    self.gain_buf.at[0, i], self.gain_buf.at[1, i], self.gain_send.at[i],
                    self.gain_recv.at[i], target,
                )
            )
        )

    def gain_finish(self, i):
        self.gain_copies[i].wait_recv()
        self.gain_buf[0, i + 1] = self.gain_buf[0, i] + self.gain_buf[1, i]

    def after(self, name):
        for part, unused, wave, slack in PARTS:
            if part == name and wave is not None:
                self.exchange(wave)
        for w, s, step in self.plan[name]:
            if step == 0 and w not in self.whole:
                self.whole.add(w)
                self.halves[w].wait()
            self.stream_step(w, s, step)
            self.count += 1
            if name == "end" and self.count % 8 == 0:
                self.gain_step()

    def gain_step(self):
        i = len(self.gain_copies)
        if i > 0 and i not in self.whole_gains:
            self.gain_finish(i - 1)
            self.whole_gains.add(i)
        if i <= self.bits:
            self.gain_start(i)

    def stream_step(self, w, s, step):
        value, core, packed, res = self.value, self.core, self.packed, self.res
        b1, b2, b3 = stream_bits(w, s)
        base = w * TILES + 4 * s
        two = base + 2 * value[b1]
        one = two + value[b2]
        half = TILE_ROWS // 2
        rows = pl.ds(pl.multiple_of(half * value[b3], 16), half)
        slot = w * STREAMS + s

        def go(src, dst, bit):
            self.flight[(slot, step)] = self.start(
                remote(
                    src, dst, self.send_sem.at[slot, step], self.recv_sem.at[slot, step],
                    (self.partner[bit], core),
                )
            )

        if step > 0:
            self.flight[(slot, step - 1)].wait_recv()
        if step == 0:
            for t in range(4):
                packed[core, base + t] = (
                    packed[core, base + t].astype(F32) + res[base + t].astype(F32)
                ).astype(BF16)
            go(packed.at[core, pl.ds(base + 2 * (1 - value[b1]), 2)], self.in1.at[slot], b1)
        elif step == 1:
            for t in range(2):
                packed[core, two + t] = (
                    packed[core, two + t].astype(F32) + self.in1[slot, t].astype(F32)
                ).astype(BF16)
            go(packed.at[core, two + 1 - value[b2]], self.in2.at[slot], b2)
        elif step == 2:
            packed[core, one] = (
                packed[core, one].astype(F32) + self.in2[slot].astype(F32)
            ).astype(BF16)
            away = pl.ds(pl.multiple_of(half * (1 - value[b3]), 16), half)
            go(packed.at[core, one, away], self.in3.at[slot], b3)
        elif step < self.bits + 1:
            at = step - 3
            own = packed[core, one, rows] if at == 0 else self.in4[slot, 0, at - 1]
            came = self.in3[slot] if at == 0 else self.in4[slot, 1, at - 1]
            total = (own.astype(F32) + came.astype(F32)).astype(BF16)
            if step < self.bits:
                self.in4[slot, 0, at] = total
                go(self.in4.at[slot, 0, at], self.in4.at[slot, 1, at], step)
            else:
                res[one, rows] = total
                go(res.at[one, rows], res.at[one, rows], b3)
        elif step == self.bits + 1:
            go(res.at[one], res.at[one], b2)
        elif step == self.bits + 2:
            go(res.at[pl.ds(two, 2)], res.at[pl.ds(two, 2)], b1)
        else:
            copy = pltpu.make_async_copy(
                res.at[pl.ds(base, 4)], self.res_out.at[pl.ds(base, 4)], self.res_sem.at[slot]
            )
            copy.start()
            self.leaving.append(copy)


def layer_kernel(
    bits, buckets,
    lengths_ref, tokens_hbm, cot_hbm, wq_hbm, wk_hbm, wv_hbm, wo_ref, wg_ref, wu_ref, wd_ref, ga_ref, gf_ref, table_hbm,
    out_hbm, dx_hbm, res_hbm, gain_out_ref,
    tokens_ref, cot_ref, wq_ref, wk_ref, wv_ref, table_ref, out_ref, dx_ref, res_ref,
    wqkv, wo, wg, wu, wd, gain_in, gain_own, gain, gain_sum, cs, bias,
    norm_one, norm_two, att, d_down, d_branch, qkv, probs, x_two, middle, hidden, d_up, d_gate,
    dn, d_att, d_qkv, packed, in1, in2, in3, in4, gain_buf,
    w_send, w_recv, w_local, half_send, half_recv, send_sem, recv_sem, gain_send, gain_recv, res_sem, in_sem, out_sem,
):
    dp = lax.axis_index("dp")
    core = lax.axis_index("fsdp")
    total = buckets * BUCKET
    red = Reduction(
        bits, dp, core, packed, res_ref, res_hbm, (in1, in2, in3, in4), gain_buf,
        (half_send, half_recv, send_sem, recv_sem, gain_send, gain_recv, res_sem),
    )
    barrier = pltpu.get_barrier_semaphore()
    for target in red.targets:
        pl.semaphore_signal(barrier, inc=1, device_id=target, device_id_type=MESH)
    inputs = [
        pltpu.make_async_copy(src, dst, in_sem.at[i])
        for i, (src, dst) in enumerate(
            [
                (wq_hbm, wq_ref), (wk_hbm, wk_ref), (wv_hbm, wv_ref), (table_hbm, table_ref), (tokens_hbm, tokens_ref),
                (cot_hbm, cot_ref),
            ]
        )
    ]
    for copy in inputs:
        copy.start()
    for copy in inputs[:3]:
        copy.wait()

    scale = 1.0 / math.sqrt(HD)
    half = pl.ds(pl.multiple_of(core * TILE_ROWS, 16), TILE_ROWS)
    down_half = pl.ds(pl.multiple_of(core * (FF // 2), 128), FF // 2)
    wqkv[half, :] = jnp.concatenate(
        [
            (wq_ref[...].astype(F32) * scale).astype(BF16),
            wk_ref[...],
            wv_ref[...],
            jnp.zeros((TILE_ROWS, QKV - D - 2 * KVW), BF16),
        ],
        axis=1,
    )
    gain_own[0:1, :TILE_ROWS] = ga_ref[...].astype(F32).reshape(1, TILE_ROWS)
    gain_own[1:2, :TILE_ROWS] = gf_ref[...].astype(F32).reshape(1, TILE_ROWS)
    pl.semaphore_wait(barrier, len(red.targets))

    whole = [
        (wqkv.at[half], wqkv.at[half]), (wo_ref, wo.at[half]), (wg_ref, wg.at[half]),
        (wu_ref, wu.at[half]), (wd_ref, wd.at[:, down_half]), (gain_own, gain_in),
    ]
    arrivals, locals_ = {}, []
    for i in (5, 0, 1, 2, 3, 4):
        src, dst = whole[i]
        arrivals[i] = red.start(remote(src, dst, w_send.at[i], w_recv.at[i], red.mate))
        if 1 <= i <= 4:
            copy = pltpu.make_async_copy(src, dst, w_local.at[i - 1])
            copy.start()
            locals_.append(copy)

    def weight(i):
        if i >= 1:
            locals_[i - 1].wait()
        arrivals[i].wait_recv()

    def lanes(b):
        return slice(b * BUCKET, (b + 1) * BUCKET)

    place = lax.broadcasted_iota(jnp.int32, (BUCKET, BUCKET), 1)
    other = lax.broadcasted_iota(jnp.int32, (BUCKET, BUCKET), 0)
    alive = []
    inputs[3].wait()
    for b in range(buckets):
        begin = jnp.zeros((BUCKET, BUCKET), jnp.int32)
        bound = 0
        for j in range(lengths_ref.shape[1]):
            bound = bound + lengths_ref[b, j]
            begin = begin + jnp.where(place >= bound, lengths_ref[b, j], 0)
        pick = jnp.where(place - begin == other, 1.0, 0.0).astype(BF16)
        parts = nn(table_ref[...], pick)
        cs[:, lanes(b)] = parts[:HD] + parts[HD : 2 * HD] + parts[2 * HD :]
        bias[b] = jnp.where((other >= begin) & (other <= place), 0.0, -1e30)
        alive.append((place[:1] < bound).astype(F32))

    inputs[4].wait()
    d_qkv[D + 2 * KVW :, :] = jnp.zeros((QKV - D - 2 * KVW, 2 * total), BF16)
    gain_sum[...] = jnp.zeros_like(gain_sum)
    gain_buf[0, 0] = jnp.zeros(gain_buf.shape[2:], F32)
    arrivals[5].wait_recv()
    wide = lax.broadcasted_iota(jnp.int32, (8, 640), 1)
    low_half = jnp.where(core == 0, gain_own[...], gain_in[...])
    high_half = jnp.where(core == 0, gain_in[...], gain_own[...])
    gains = jnp.where(wide < TILE_ROWS, low_half, pltpu.roll(high_half, TILE_ROWS, 1))
    for i in range(2):
        gain[i] = jnp.broadcast_to(gains[i : i + 1, :D], (BUCKET, D)).T

    def x_of(p, b, rows=slice(None)):
        if p == 0:
            return tokens_ref[b, rows, :].astype(F32)
        return x_two[rows, lanes(b)]

    def middle_of(p, b, rows=slice(None)):
        return middle[p, rows, lanes(b)]

    def norm_forward(p, read, i, dst):
        for b in range(buckets):
            x = read(p, b)
            inv = lax.rsqrt(jnp.sum(x * x, axis=0, keepdims=True) * (1.0 / D) + 1e-05)
            dst[:, lanes(p * buckets + b)] = (x * inv * gain[i]).astype(BF16)

    def norm_backward(p, read, i, low_to):
        block = 64
        stats = []
        for b in range(buckets):
            squares = jnp.zeros((8, BUCKET), F32)
            dots = jnp.zeros((8, BUCKET), F32)
            for k in range(0, D, block):
                rows = slice(k, k + block)
                x = read(p, b, rows)
                d = dn[rows, lanes(b)] * gain[i, rows, :]
                squares = squares + jnp.sum((x * x).reshape(block // 8, 8, BUCKET), axis=0)
                dots = dots + jnp.sum((d * x).reshape(block // 8, 8, BUCKET), axis=0)
            inv = lax.rsqrt(jnp.sum(squares, axis=0, keepdims=True) * (1.0 / D) + 1e-05)
            mean = jnp.sum(dots, axis=0, keepdims=True) * inv * (1.0 / D)
            stats.append((inv, mean))
        for k in range(0, D, block):
            rows = slice(k, k + block)
            gain_term = gain_sum[i, rows, :]
            for b in range(buckets):
                inv, mean = stats[b]
                hat = read(p, b, rows) * inv
                d = dn[rows, lanes(b)]
                gain_term = gain_term + d * hat
                new = dx_ref[b, rows, :] + inv * (d * gain[i, rows, :] - hat * mean)
                dx_ref[b, rows, :] = new
                if low_to is not None:
                    low_to[rows, lanes(b)] = new.astype(BF16)
            gain_sum[i, rows, :] = gain_term

    def rope(z, b, sign):
        first, second = z[: HD // 2], z[HD // 2 :]
        cosines, sines = cs[: HD // 2, lanes(b)], cs[HD // 2 :, lanes(b)]
        if sign < 0:
            return jnp.concatenate([first * cosines + second * sines, second * cosines - first * sines], axis=0)
        return jnp.concatenate([first * cosines - second * sines, second * cosines + first * sines], axis=0)

    def head(h):
        return slice(HD * h, HD * (h + 1))

    def key_head(g):
        return head(HEADS + g)

    def value_head(g):
        return head(HEADS + KV_HEADS + g)

    def three(ref, g, where):
        return jnp.concatenate([ref[head(h), where] for h in range(GROUP * g, GROUP * (g + 1))], axis=1)

    def forward(p):
        at = slice(p * total, (p + 1) * total)
        norm_forward(p, x_of, 0, norm_one)
        if p == 0:
            weight(0)
        z = tn(wqkv[:, : D + 2 * KVW], norm_one[:, at])
        for h in range(HEADS + KV_HEADS):
            for b in range(buckets):
                qkv[head(h), lanes(p * buckets + b)] = rope(z[head(h), lanes(b)], b, 1).astype(BF16)
        qkv[D + KVW :, at] = z[D + KVW :].astype(BF16)
        todo = [(b, g) for b in range(buckets) for g in range(KV_HEADS)]
        for first in range(0, len(todo), ATTEND):
            part = [(b, g, lanes(p * buckets + b)) for b, g in todo[first : first + ATTEND]]
            scores = [
                tn(qkv[key_head(g), here], three(qkv, g, here)) + jnp.concatenate([bias[b]] * GROUP, axis=1)
                for b, g, here in part
            ]
            lows = []
            for (b, g, here), score in zip(part, scores):
                e = jnp.exp(score - jnp.max(score, axis=0, keepdims=True))
                low = (e * (1.0 / jnp.sum(e, axis=0, keepdims=True))).astype(BF16)
                probs[p * buckets + b, g] = low
                lows.append(low)
            for (b, g, here), low in zip(part, lows):
                mixed = nn(qkv[value_head(g), here], low).astype(BF16)
                for i in range(GROUP):
                    att[head(GROUP * g + i), here] = mixed[:, lanes(i)]
        if p == 0:
            weight(1)
        mixed = tn(wo[...], att[:, at])
        for b in range(buckets):
            middle[p, :, lanes(b)] = x_of(p, b) + mixed[:, lanes(b)]
        norm_forward(p, middle_of, 1, norm_two)
        if p == 0:
            weight(2)
            weight(3)
        for c in range(0, FF, CHUNK):
            rows = slice(c, c + CHUNK)
            gate = tn(wg[:, rows], norm_two[:, at])
            up = tn(wu[:, rows], norm_two[:, at])
            s = 1.0 / (1.0 + jnp.exp(-gate))
            silu = gate * s
            hidden[rows, at] = (silu * up).astype(BF16)
            d_up[rows, at] = silu.astype(BF16)
            d_gate[rows, at] = (up * (s + silu * (1.0 - s))).astype(BF16)
        if p == 0:
            weight(4)
        result = middle[p] + nn(wd[...], hidden[:, at])
        if p == 0:
            x_two[...] = result
        else:
            inputs[5].wait()
            for b in range(buckets):
                out_ref[b] = (result[:, lanes(b)] * alive[b]).astype(BF16)
                grad = cot_ref[b].astype(F32) * alive[b]
                dx_ref[b] = grad
                d_down[:, lanes(buckets + b)] = grad.astype(BF16)

    def put(first, block):
        low = block.astype(BF16)
        for h in range(2):
            for j in range(2):
                packed[h, first + j] = low[TILE_ROWS * h : TILE_ROWS * (h + 1), 128 * j : 128 * (j + 1)]

    def grad_down(h):
        per = FF // 2 // CHUNK
        for c in range(per):
            rows = pl.ds(pl.multiple_of(h * (FF // 2) + c * CHUNK, CHUNK), CHUNK)
            low = nt(d_down[...], hidden[rows, :]).astype(BF16)
            for i in range(2):
                for j in range(2):
                    packed[h, 6 * i + 2 * c + j] = low[TILE_ROWS * i : TILE_ROWS * (i + 1), 128 * j : 128 * (j + 1)]

    def grad_ffn(wave, d, part):
        for c in range(3 * part, 3 * part + 3):
            put(wave * TILES + 2 * c, nt(norm_two[...], d[c * CHUNK : (c + 1) * CHUNK, :]))

    def backward(p):
        at = slice(p * total, (p + 1) * total)
        if p == 0:
            grad_down(1 - core)
            red.after("down_a")
            grad_down(core)
            red.after("down_b")
        for c in range(0, FF, CHUNK):
            rows = slice(c, c + CHUNK)
            d_hidden = tn(wd[:, rows], d_down[:, at])
            d_up[rows, at] = (d_hidden * d_up[rows, at].astype(F32)).astype(BF16)
            d_gate[rows, at] = (d_hidden * d_gate[rows, at].astype(F32)).astype(BF16)
        if p == 0:
            red.after("gated")
            for wave, d, name in ((1, d_gate, "gate"), (2, d_up, "up")):
                grad_ffn(wave, d, 0)
                red.after(name + "_a")
                grad_ffn(wave, d, 1)
                red.after(name + "_b")
        dn[...] = nn(wg[...], d_gate[:, at]) + nn(wu[...], d_up[:, at])
        if p == 0:
            red.after("ffn")
        norm_backward(p, middle_of, 1, d_branch.at[:, at])
        if p == 0:
            red.after("norm_two")
        d_att[...] = nn(wo[...], d_branch[:, at]).astype(BF16)
        if p == 0:
            red.after("branch")
        todo = [(b, g) for b in range(buckets) for g in range(KV_HEADS)]
        for first in range(0, len(todo), ATTEND):
            part = todo[first : first + ATTEND]
            d_probs = [
                tn(qkv[value_head(g), lanes(p * buckets + b)], three(d_att, g, lanes(b))) for b, g in part
            ]
            d_scores = []
            for (b, g), d in zip(part, d_probs):
                pr = probs[p * buckets + b, g].astype(F32)
                d_scores.append((pr * (d - jnp.sum(d * pr, axis=0, keepdims=True))).astype(BF16))
            for (b, g), ds in zip(part, d_scores):
                here = lanes(p * buckets + b)
                d_query = nn(qkv[key_head(g), here], ds)
                for i in range(GROUP):
                    d_qkv[head(GROUP * g + i), here] = rope(d_query[:, lanes(i)], b, -1).astype(BF16)
                d_qkv[key_head(g), here] = rope(nt(three(qkv, g, here), ds), b, -1).astype(BF16)
                d_qkv[value_head(g), here] = nt(
                    three(d_att, g, lanes(b)), probs[p * buckets + b, g]
                ).astype(BF16)
            if p == 0:
                red.after("scores_a" if first == 0 else "scores_b")

    def backward_end(p):
        dn[...] = nn(wqkv[...], d_qkv[:, p * total : (p + 1) * total])
        if p == 0:
            red.after("qkv")
        norm_backward(p, x_of, 0, d_down.at[:, :total] if p == 1 else None)

    forward(0)
    forward(1)
    results = [pltpu.make_async_copy(out_ref, out_hbm, out_sem.at[0])]
    results[0].start()
    backward(1)
    backward_end(1)
    backward(0)

    column = lax.broadcasted_iota(jnp.int32, (1, CHUNK), 1)
    for c in range(3):
        block = nt(norm_one[...], d_qkv[c * CHUNK : (c + 1) * CHUNK, :])
        put(3 * TILES + 2 * c, block * jnp.where(column + c * CHUNK < D, scale, 1.0))
    block = nt(norm_one[...], d_qkv[3 * CHUNK :, :])
    rest = nt(att[...], d_branch[2 * CHUNK :, :])
    put(3 * TILES + 6, jnp.concatenate([block[:, : D + 2 * KVW - 3 * CHUNK], rest], axis=1))
    for c in range(2):
        put(3 * TILES + 8 + 2 * c, nt(att[...], d_branch[c * CHUNK : (c + 1) * CHUNK, :]))
    red.after("rest")
    backward_end(0)
    results.append(pltpu.make_async_copy(dx_ref, dx_hbm, out_sem.at[1]))
    results[1].start()
    for i in range(2):
        gain_buf[0, 0, i : i + 1, :D] = jnp.sum(gain_sum[i].T, axis=0, keepdims=True)
    red.gain_step()
    red.after("norm_one")
    red.after("end")
    while len(red.whole_gains) <= bits:
        red.gain_step()
    sums = gain_buf[0, bits + 1]
    gain_out_ref[...] = jnp.where(core == 0, sums, pltpu.roll(sums, 640 - TILE_ROWS, 1))
    for copy in red.started:
        copy.wait_send()
    for copy in results + red.leaving:
        copy.wait()


def run_layer(bits, lengths, tokens, cotangent, weights, gains):
    buckets = tokens.shape[0]
    total = buckets * BUCKET
    slots = WAVES * STREAMS
    half = (TILE_ROWS // 2, 128)
    steps = bits + 3
    vmem = pl.BlockSpec(memory_space=pltpu.VMEM)
    hbm = pl.BlockSpec(memory_space=pl.ANY)
    dma = pltpu.SemaphoreType.DMA
    grads = (WAVES * TILES, TILE_ROWS, 128)
    table = jnp.asarray(rope_table())
    scratch = [
        (tokens.shape, BF16), (tokens.shape, BF16), *((w.shape, BF16) for w in weights[:3]), (table.shape, BF16),
        (tokens.shape, BF16), (tokens.shape, F32), (grads, BF16),
        ((D, QKV), BF16), ((D, D), BF16), ((D, FF), BF16), ((D, FF), BF16), ((D, FF), BF16),
        ((8, 640), F32), ((8, 640), F32), ((2, D, BUCKET), F32), ((2, D, BUCKET), F32),
        ((HD, total), F32), ((buckets, BUCKET, BUCKET), F32),
        ((D, 2 * total), BF16), ((D, 2 * total), BF16), ((D, 2 * total), BF16),
        ((D, 2 * total), BF16), ((D, 2 * total), BF16),
        ((D + 2 * KVW, 2 * total), BF16),
        ((2 * buckets, KV_HEADS, BUCKET, GROUP * BUCKET), BF16),
        ((D, total), F32), ((2, D, total), F32),
        ((FF, 2 * total), BF16), ((FF, 2 * total), BF16), ((FF, 2 * total), BF16),
        ((D, total), F32), ((D, total), BF16), ((QKV, 2 * total), BF16),
        ((2, *grads), BF16), ((slots, 2, TILE_ROWS, 128), BF16), ((slots, TILE_ROWS, 128), BF16),
        ((slots, *half), BF16), ((slots, 2, bits - 3, *half), BF16), ((2, bits + 2, 8, 640), F32),
    ]
    return pl.pallas_call(
        functools.partial(layer_kernel, bits, buckets),
        out_shape=(
            jax.ShapeDtypeStruct((buckets, D, BUCKET), BF16),
            jax.ShapeDtypeStruct((buckets, D, BUCKET), F32),
            jax.ShapeDtypeStruct(grads, BF16),
            jax.ShapeDtypeStruct((8, 640), F32),
        ),
        in_specs=[pl.BlockSpec(memory_space=pltpu.SMEM)] + [hbm] * 9 + [vmem] * 2 + [hbm],
        out_specs=(hbm,) * 3 + (vmem,),
        scratch_shapes=[pltpu.VMEM(shape, dtype) for shape, dtype in scratch]
        + [
            dma((6,)), dma((6,)), dma((4,)), dma((WAVES,)), dma((WAVES,)), dma((slots, steps)),
            dma((slots, steps)), dma((bits + 1,)), dma((bits + 1,)), dma((slots,)), dma((6,)), dma((2,)),
        ],
        compiler_params=pltpu.CompilerParams(
            collective_id=0, has_side_effects=True, vmem_limit_bytes=63 << 20
        ),
    )(lengths, tokens, cotangent, *weights, *gains, table)


def unpack_kernel(
    res_hbm, out_in, dx_in, gain_in,
    out_ref, dx_ref, gq, gk, gv, go, gg, gu, gd, ga, gf,
    res_ref, out_block, dx_block, query, key, value, branch, gate, up, down, in_sem, out_sem,
):
    arrivals = [
        pltpu.make_async_copy(res_hbm.at[pl.ds(w * TILES, TILES)], res_ref.at[pl.ds(w * TILES, TILES)], in_sem.at[w])
        for w in range(WAVES)
    ]
    arrivals.append(pltpu.make_async_copy(dx_in, dx_block, in_sem.at[WAVES]))
    arrivals.append(pltpu.make_async_copy(out_in, out_block, in_sem.at[WAVES + 1]))
    for copy in arrivals:
        copy.start()
    copies = []
    ga[...] = gain_in[0, :TILE_ROWS]
    gf[...] = gain_in[1, :TILE_ROWS]

    def tile(t):
        return res_ref[t].astype(F32)

    def leave(src, dst):
        copy = pltpu.make_async_copy(src, dst, out_sem.at[len(copies)])
        copy.start()
        copies.append(copy)

    arrivals[0].wait()
    for j in range(6):
        for h in range(2):
            down[TILE_ROWS * h : TILE_ROWS * (h + 1), 128 * j : 128 * (j + 1)] = tile(6 * h + j)
    leave(down, gd)
    for w, block, dst in ((1, gate, gg), (2, up, gu)):
        arrivals[w].wait()
        for j in range(TILES):
            block[:, 128 * j : 128 * (j + 1)] = tile(w * TILES + j)
        leave(block, dst)
    arrivals[3].wait()
    first = 3 * TILES
    for j in range(4):
        query[:, 128 * j : 128 * (j + 1)] = tile(first + j)
        branch[:, 128 * j : 128 * (j + 1)] = tile(first + 8 + j)
    shared, last = tile(first + 4), tile(first + 7)
    query[:, 512:] = shared[:, :64]
    leave(query, gq)
    branch[:, 512:] = last[:, 64:]
    leave(branch, go)
    key[...] = jnp.concatenate([shared[:, 64:], tile(first + 5)], axis=1)
    leave(key, gk)
    value[...] = jnp.concatenate([tile(first + 6), last[:, :64]], axis=1)
    leave(value, gv)
    arrivals[WAVES].wait()
    leave(dx_block, dx_ref)
    arrivals[WAVES + 1].wait()
    leave(out_block, out_ref)
    for copy in copies:
        copy.wait()


def unpack(res, output, input_grad, gain_sum):
    shapes = [
        (TILE_ROWS, D), (TILE_ROWS, KVW), (TILE_ROWS, KVW), (TILE_ROWS, D), (TILE_ROWS, FF), (TILE_ROWS, FF),
        (D, FF // 2),
    ]
    vmem = pl.BlockSpec(memory_space=pltpu.VMEM)
    hbm = pl.BlockSpec(memory_space=pl.ANY)
    dma = pltpu.SemaphoreType.DMA
    return pl.pallas_call(
        unpack_kernel,
        out_shape=(
            jax.ShapeDtypeStruct(output.shape, output.dtype),
            jax.ShapeDtypeStruct(input_grad.shape, input_grad.dtype),
            *(jax.ShapeDtypeStruct(shape, F32) for shape in shapes + [(TILE_ROWS,)] * 2),
        ),
        in_specs=[hbm] * 3 + [vmem],
        out_specs=(hbm,) * 9 + (vmem,) * 2,
        scratch_shapes=[pltpu.VMEM(a.shape, a.dtype) for a in (res, output, input_grad)]
        + [pltpu.VMEM(shape, F32) for shape in shapes]
        + [dma((WAVES + 2,)), dma((len(shapes) + 2,))],
        compiler_params=pltpu.CompilerParams(vmem_limit_bytes=63 << 20),
    )(res, output, input_grad, gain_sum)


def on_device(
    bits, tokens, cotangent, lengths, w_query, w_key, w_value, w_out, w_gate, w_up, w_down, gain_attn, gain_ffn,
):
    output, input_grad, res, gain_sum = run_layer(
        bits,
        lengths[:, 0],
        tokens[:, 0].transpose(0, 2, 1),
        cotangent[:, 0].transpose(0, 2, 1),
        (w_query, w_key, w_value, w_out, w_gate, w_up, w_down.T),
        (gain_attn, gain_ffn),
    )
    output, input_grad, gq, gk, gv, go, gg, gu, gd, ga, gf = unpack(res, output, input_grad, gain_sum)
    return (
        output.transpose(0, 2, 1)[:, None], input_grad.transpose(0, 2, 1)[:, None],
        gq, gk, gv, go, gg, gu, gd.T, ga, gf,
    )


def solution(mesh):
    rows = P(None, ("dp", "fsdp"), None, None)
    weight = P("fsdp", None)
    in_specs = (rows, rows, P(None, ("dp", "fsdp"), None)) + (weight,) * 7 + (P("fsdp"),) * 2
    out_specs = (rows, rows) + (weight,) * 7 + (P("fsdp"),) * 2
    bits = mesh.shape["dp"].bit_length() - 1
    return jax.shard_map(
        functools.partial(on_device, bits),
        mesh=mesh,
        in_specs=in_specs,
        out_specs=out_specs,
        check_vma=False,
    )
```

```python
import functools
import math

import jax
import jax.numpy as jnp
import ml_dtypes
import numpy as np
from jax import lax
from jax.experimental import pallas as pl
from jax.experimental.pallas import tpu as pltpu
from jax.sharding import PartitionSpec as P

HEADS = 9
KV_HEADS = 3
GROUP = HEADS // KV_HEADS
HD = 64
D = 576
FF = 1536
KVW = KV_HEADS * HD
BUCKET = 128
MESH = pl.DeviceIdType.MESH
F32 = jnp.float32
BF16 = jnp.bfloat16

WAVES = 4
STREAMS = 3
TILES = 4 * STREAMS
TILE_ROWS = 288
QKV = 1024
CHUNK = 256
ATTEND = 6


def nn(a, b):
    return lax.dot_general(a, b, (((1,), (0,)), ((), ())), preferred_element_type=F32)


def nt(a, b):
    return lax.dot_general(a, b, (((1,), (1,)), ((), ())), preferred_element_type=F32)


def tn(a, b):
    return lax.dot_general(a, b, (((0,), (0,)), ((), ())), preferred_element_type=F32)


def rope_table():
    inverse = np.exp(np.arange(HD // 2) * (-2.0 * math.log(10000.0) / HD))
    angles = inverse[:, None] * np.arange(BUCKET)[None, :]
    rest = np.concatenate([np.cos(angles), np.sin(angles)], axis=0)
    parts = []
    for unused in range(3):
        part = rest.astype(ml_dtypes.bfloat16)
        parts.append(part)
        rest = rest - part.astype(np.float64)
    return np.concatenate(parts, axis=0)


STREAM_BITS = (
    ((2, 1, 0), (0, 2, 1), (1, 0, 2)),
    ((2, 0, 1), (0, 2, 1), (1, 0, 2)),
    ((0, 1, 2), (2, 1, 0), (1, 2, 0)),
    ((2, 1, 0), (1, 0, 2), (0, 2, 1)),
)


def stream_bits(wave, stream):
    return STREAM_BITS[wave][stream]


TILE_TIME, STEP_TIME, WAVE_TIME, WAVE_STEP_TIME = 1.42, 2.65, 1.3, 1.5
STEP_RANK, WAVE_RANK, THIRD_RANK = 11.420752228273008, 10.744307844872964, -0.1535938302871354
PARTS = (
    ("down_a", 1.05, 0, -5.0), ("down_b", 1.05, None, -5.0), ("gated", 1.7, None, 0.0), ("gate_a", 1.05, None, -1.0),
    ("gate_b", 1.05, 1, 0.3), ("up_a", 1.05, None, 0.3), ("up_b", 1.05, 2, 0.6), ("ffn", 2.1, None, 1.0),
    ("norm_two", 0.75, None, 0.0), ("branch", 0.7, None, -1.0), ("scores_a", 1.0, None, 0.6),
    ("scores_b", 1.0, None, 0.3), ("rest", 2.1, 3, 0.6), ("qkv", 0.85, None, 0.6), ("norm_one", 1.1, None, 0.0),
    ("end", 0.0, None, 1e9),
)


def plan_steps(bits):
    last = bits + 3
    free = {"core": 0.0, 0: 0.0, 1: 0.0, 2: 0.0, "far": 0.0}
    waiting, plan, now = {}, {}, 0.0

    def sent(w, s, k):
        b1, b2, b3 = stream_bits(w, s)
        links = {0: (b1, 2), 1: (b2, 1), 2: (b3, 0.5), bits: (b3, 0.5), bits + 1: (b2, 1), bits + 2: (b1, 2)}
        link, tiles = links.get(k, ("far", 0.5))
        time = tiles * TILE_TIME
        if link == "far":
            begin = max(now, free[2])
            free[2] = begin + time
            free["far"] = max(begin, free["far"]) + 2 * time
            return free["far"] + STEP_TIME + 0.6
        free[link] = max(now, free[link]) + time
        return free[link] + STEP_TIME

    for name, time, wave, slack in PARTS:
        now += time
        limit = now + slack
        steps = plan[name] = []
        if wave is not None:
            free["core"] = max(now, free["core"]) + WAVE_TIME
            waiting.update({(wave, s): (free["core"] + WAVE_STEP_TIME, 0) for s in range(STREAMS)})
        while True:
            ranked = [
                (max(came, now) + STEP_RANK * k + WAVE_RANK * w + THIRD_RANK * (s == 2), came, w, s, k)
                for (w, s), (came, k) in waiting.items()
                if came <= limit
            ]
            if not ranked:
                break
            unused, came, w, s, k = min(ranked)
            now = max(now, came) + 0.2
            steps.append((w, s, k))
            if k < last:
                waiting[w, s] = (sent(w, s, k), k + 1)
            else:
                del waiting[w, s]
    return plan


def remote(src, dst, send, recv, target):
    return pltpu.make_async_remote_copy(
        src_ref=src, dst_ref=dst, send_sem=send, recv_sem=recv, device_id=target,
        device_id_type=MESH,
    )


class Reduction:
    def __init__(self, bits, dp, core, packed, res, res_out, ins, gain_buf, sems):
        self.bits, self.core, self.packed, self.res, self.res_out = bits, core, packed, res, res_out
        self.in1, self.in2, self.in3, self.in4 = ins
        self.gain_buf = gain_buf
        (
            self.half_send, self.half_recv, self.send_sem, self.recv_sem, self.gain_send, self.gain_recv, self.res_sem,
        ) = sems
        self.value = [(dp // (1 << b)) % 2 for b in range(bits)]
        self.partner = [dp + (1 << b) * (1 - 2 * self.value[b]) for b in range(bits)]
        self.mate = (dp, 1 - core)
        self.targets = [self.mate] + [(self.partner[b], core) for b in range(bits)]
        self.last = bits + 3
        self.started, self.flight, self.halves, self.gain_copies, self.leaving = [], {}, {}, [], []
        self.plan, self.whole, self.whole_gains, self.count = plan_steps(bits), set(), set(), 0

    def start(self, copy):
        copy.start()
        self.started.append(copy)
        return copy

    def exchange(self, w):
        tiles = pl.ds(w * TILES, TILES)
        self.halves[w] = remote(
            self.packed.at[1 - self.core, tiles], self.res.at[tiles],
            self.half_send.at[w], self.half_recv.at[w], self.mate,
        )
        self.halves[w].start()

    def gain_start(self, i):
        target = self.targets[i]
        self.gain_copies.append(
            self.start(
                remote(
                    self.gain_buf.at[0, i], self.gain_buf.at[1, i], self.gain_send.at[i],
                    self.gain_recv.at[i], target,
                )
            )
        )

    def gain_finish(self, i):
        self.gain_copies[i].wait_recv()
        self.gain_buf[0, i + 1] = self.gain_buf[0, i] + self.gain_buf[1, i]

    def after(self, name):
        for part, unused, wave, slack in PARTS:
            if part == name and wave is not None:
                self.exchange(wave)
        for w, s, step in self.plan[name]:
            if step == 0 and w not in self.whole:
                self.whole.add(w)
                self.halves[w].wait()
            self.stream_step(w, s, step)
            self.count += 1
            if name == "end" and self.count % 11 == 0:
                self.gain_step()

    def gain_step(self):
        i = len(self.gain_copies)
        if i > 0 and i not in self.whole_gains:
            self.gain_finish(i - 1)
            self.whole_gains.add(i)
        if i <= self.bits:
            self.gain_start(i)

    def stream_step(self, w, s, step):
        value, core, packed, res = self.value, self.core, self.packed, self.res
        b1, b2, b3 = stream_bits(w, s)
        base = w * TILES + 4 * s
        two = base + 2 * value[b1]
        one = two + value[b2]
        half = TILE_ROWS // 2
        rows = pl.ds(pl.multiple_of(half * value[b3], 16), half)
        slot = w * STREAMS + s

        def go(src, dst, bit):
            self.flight[(slot, step)] = self.start(
                remote(
                    src, dst, self.send_sem.at[slot, step], self.recv_sem.at[slot, step],
                    (self.partner[bit], core),
                )
            )

        if step > 0:
            self.flight[(slot, step - 1)].wait_recv()
        if step == 0:
            for t in range(4):
                packed[core, base + t] = (
                    packed[core, base + t].astype(F32) + res[base + t].astype(F32)
                ).astype(BF16)
            go(packed.at[core, pl.ds(base + 2 * (1 - value[b1]), 2)], self.in1.at[slot], b1)
        elif step == 1:
            for t in range(2):
                packed[core, two + t] = (
                    packed[core, two + t].astype(F32) + self.in1[slot, t].astype(F32)
                ).astype(BF16)
            go(packed.at[core, two + 1 - value[b2]], self.in2.at[slot], b2)
        elif step == 2:
            packed[core, one] = (
                packed[core, one].astype(F32) + self.in2[slot].astype(F32)
            ).astype(BF16)
            away = pl.ds(pl.multiple_of(half * (1 - value[b3]), 16), half)
            go(packed.at[core, one, away], self.in3.at[slot], b3)
        elif step < self.bits + 1:
            at = step - 3
            own = packed[core, one, rows] if at == 0 else self.in4[slot, 0, at - 1]
            came = self.in3[slot] if at == 0 else self.in4[slot, 1, at - 1]
            total = (own.astype(F32) + came.astype(F32)).astype(BF16)
            if step < self.bits:
                self.in4[slot, 0, at] = total
                go(self.in4.at[slot, 0, at], self.in4.at[slot, 1, at], step)
            else:
                res[one, rows] = total
                go(res.at[one, rows], res.at[one, rows], b3)
        elif step == self.bits + 1:
            go(res.at[one], res.at[one], b2)
        elif step == self.bits + 2:
            go(res.at[pl.ds(two, 2)], res.at[pl.ds(two, 2)], b1)
        else:
            copy = pltpu.make_async_copy(
                res.at[pl.ds(base, 4)], self.res_out.at[pl.ds(base, 4)], self.res_sem.at[slot]
            )
            copy.start()
            self.leaving.append(copy)


def layer_kernel(
    bits, buckets,
    lengths_ref, tokens_hbm, cot_hbm, wq_hbm, wk_hbm, wv_hbm, wo_ref, wg_ref, wu_ref, wd_ref, ga_ref, gf_ref, table_hbm,
    out_hbm, dx_hbm, res_hbm, gain_out_ref,
    tokens_ref, cot_ref, wq_ref, wk_ref, wv_ref, table_ref, out_ref, dx_ref, res_ref,
    wqkv, wo, wg, wu, wd, gain_in, gain_own, gain, gain_sum, cs, bias,
    norm_one, norm_two, att, d_down, d_branch, qkv, probs, x_two, middle, hidden, d_up, d_gate,
    dn, d_att, d_qkv, packed, in1, in2, in3, in4, gain_buf,
    w_send, w_recv, w_local, half_send, half_recv, send_sem, recv_sem, gain_send, gain_recv, res_sem, in_sem, out_sem,
):
    dp = lax.axis_index("dp")
    core = lax.axis_index("fsdp")
    total = buckets * BUCKET
    red = Reduction(
        bits, dp, core, packed, res_ref, res_hbm, (in1, in2, in3, in4), gain_buf,
        (half_send, half_recv, send_sem, recv_sem, gain_send, gain_recv, res_sem),
    )
    barrier = pltpu.get_barrier_semaphore()
    for target in red.targets:
        pl.semaphore_signal(barrier, inc=1, device_id=target, device_id_type=MESH)
    inputs = [
        pltpu.make_async_copy(src, dst, in_sem.at[i])
        for i, (src, dst) in enumerate(
            [
                (wq_hbm, wq_ref), (wk_hbm, wk_ref), (wv_hbm, wv_ref), (table_hbm, table_ref), (tokens_hbm, tokens_ref),
                (cot_hbm, cot_ref),
            ]
        )
    ]
    for copy in inputs:
        copy.start()
    for copy in inputs[:3]:
        copy.wait()

    scale = 1.0 / math.sqrt(HD)
    half = pl.ds(pl.multiple_of(core * TILE_ROWS, 16), TILE_ROWS)
    down_half = pl.ds(pl.multiple_of(core * (FF // 2), 128), FF // 2)
    wqkv[half, :] = jnp.concatenate(
        [
            (wq_ref[...].astype(F32) * scale).astype(BF16),
            wk_ref[...],
            wv_ref[...],
            jnp.zeros((TILE_ROWS, QKV - D - 2 * KVW), BF16),
        ],
        axis=1,
    )
    gain_own[0:1, :TILE_ROWS] = ga_ref[...].astype(F32).reshape(1, TILE_ROWS)
    gain_own[1:2, :TILE_ROWS] = gf_ref[...].astype(F32).reshape(1, TILE_ROWS)
    pl.semaphore_wait(barrier, len(red.targets))

    whole = [
        (wqkv.at[half], wqkv.at[half]), (wo_ref, wo.at[half]), (wg_ref, wg.at[half]),
        (wu_ref, wu.at[half]), (wd_ref, wd.at[:, down_half]), (gain_own, gain_in),
    ]
    arrivals, locals_ = {}, []
    for i in (5, 0, 1, 2, 3, 4):
        src, dst = whole[i]
        arrivals[i] = red.start(remote(src, dst, w_send.at[i], w_recv.at[i], red.mate))
        if 1 <= i <= 4:
            copy = pltpu.make_async_copy(src, dst, w_local.at[i - 1])
            copy.start()
            locals_.append(copy)

    def weight(i):
        if i >= 1:
            locals_[i - 1].wait()
        arrivals[i].wait_recv()

    def lanes(b):
        return slice(b * BUCKET, (b + 1) * BUCKET)

    place = lax.broadcasted_iota(jnp.int32, (BUCKET, BUCKET), 1)
    other = lax.broadcasted_iota(jnp.int32, (BUCKET, BUCKET), 0)
    alive = []
    inputs[3].wait()
    for b in range(buckets):
        begin = jnp.zeros((BUCKET, BUCKET), jnp.int32)
        bound = 0
        for j in range(lengths_ref.shape[1]):
            bound = bound + lengths_ref[b, j]
            begin = begin + jnp.where(place >= bound, lengths_ref[b, j], 0)
        pick = jnp.where(place - begin == other, 1.0, 0.0).astype(BF16)
        parts = nn(table_ref[...], pick)
        cs[:, lanes(b)] = parts[:HD] + parts[HD : 2 * HD] + parts[2 * HD :]
        bias[b] = jnp.where((other >= begin) & (other <= place), 0.0, -1e30)
        alive.append((place[:1] < bound).astype(F32))

    inputs[4].wait()
    d_qkv[D + 2 * KVW :, :] = jnp.zeros((QKV - D - 2 * KVW, 2 * total), BF16)
    gain_sum[...] = jnp.zeros_like(gain_sum)
    gain_buf[0, 0] = jnp.zeros(gain_buf.shape[2:], F32)
    arrivals[5].wait_recv()
    wide = lax.broadcasted_iota(jnp.int32, (8, 640), 1)
    low_half = jnp.where(core == 0, gain_own[...], gain_in[...])
    high_half = jnp.where(core == 0, gain_in[...], gain_own[...])
    gains = jnp.where(wide < TILE_ROWS, low_half, pltpu.roll(high_half, TILE_ROWS, 1))
    for i in range(2):
        gain[i] = jnp.broadcast_to(gains[i : i + 1, :D], (BUCKET, D)).T

    def x_of(p, b, rows=slice(None)):
        if p == 0:
            return tokens_ref[b, rows, :].astype(F32)
        return x_two[rows, lanes(b)]

    def middle_of(p, b, rows=slice(None)):
        return middle[p, rows, lanes(b)]

    def norm_forward(p, read, i, dst):
        for b in range(buckets):
            x = read(p, b)
            inv = lax.rsqrt(jnp.sum(x * x, axis=0, keepdims=True) * (1.0 / D) + 1e-05)
            dst[:, lanes(p * buckets + b)] = (x * inv * gain[i]).astype(BF16)

    def norm_backward(p, read, i, low_to):
        block = 64
        stats = []
        for b in range(buckets):
            squares = jnp.zeros((8, BUCKET), F32)
            dots = jnp.zeros((8, BUCKET), F32)
            for k in range(0, D, block):
                rows = slice(k, k + block)
                x = read(p, b, rows)
                d = dn[rows, lanes(b)] * gain[i, rows, :]
                squares = squares + jnp.sum((x * x).reshape(block // 8, 8, BUCKET), axis=0)
                dots = dots + jnp.sum((d * x).reshape(block // 8, 8, BUCKET), axis=0)
            inv = lax.rsqrt(jnp.sum(squares, axis=0, keepdims=True) * (1.0 / D) + 1e-05)
            mean = jnp.sum(dots, axis=0, keepdims=True) * inv * (1.0 / D)
            stats.append((inv, mean))
        for k in range(0, D, block):
            rows = slice(k, k + block)
            gain_term = gain_sum[i, rows, :]
            for b in range(buckets):
                inv, mean = stats[b]
                hat = read(p, b, rows) * inv
                d = dn[rows, lanes(b)]
                gain_term = gain_term + d * hat
                new = dx_ref[b, rows, :] + inv * (d * gain[i, rows, :] - hat * mean)
                dx_ref[b, rows, :] = new
                if low_to is not None:
                    low_to[rows, lanes(b)] = new.astype(BF16)
            gain_sum[i, rows, :] = gain_term

    def rope(z, b, sign):
        first, second = z[: HD // 2], z[HD // 2 :]
        cosines, sines = cs[: HD // 2, lanes(b)], cs[HD // 2 :, lanes(b)]
        if sign < 0:
            return jnp.concatenate([first * cosines + second * sines, second * cosines - first * sines], axis=0)
        return jnp.concatenate([first * cosines - second * sines, second * cosines + first * sines], axis=0)

    def head(h):
        return slice(HD * h, HD * (h + 1))

    def key_head(g):
        return head(HEADS + g)

    def value_head(g):
        return head(HEADS + KV_HEADS + g)

    def three(ref, g, where):
        return jnp.concatenate([ref[head(h), where] for h in range(GROUP * g, GROUP * (g + 1))], axis=1)

    def forward(p):
        at = slice(p * total, (p + 1) * total)
        norm_forward(p, x_of, 0, norm_one)
        if p == 0:
            weight(0)
        z = tn(wqkv[:, : D + 2 * KVW], norm_one[:, at])
        for h in range(HEADS + KV_HEADS):
            for b in range(buckets):
                qkv[head(h), lanes(p * buckets + b)] = rope(z[head(h), lanes(b)], b, 1).astype(BF16)
        qkv[D + KVW :, at] = z[D + KVW :].astype(BF16)
        todo = [(b, g) for b in range(buckets) for g in range(KV_HEADS)]
        for first in range(0, len(todo), ATTEND):
            part = [(b, g, lanes(p * buckets + b)) for b, g in todo[first : first + ATTEND]]
            scores = [
                tn(qkv[key_head(g), here], three(qkv, g, here)) + jnp.concatenate([bias[b]] * GROUP, axis=1)
                for b, g, here in part
            ]
            lows = []
            for (b, g, here), score in zip(part, scores):
                e = jnp.exp(score - jnp.max(score, axis=0, keepdims=True))
                low = (e * (1.0 / jnp.sum(e, axis=0, keepdims=True))).astype(BF16)
                probs[p * buckets + b, g] = low
                lows.append(low)
            for (b, g, here), low in zip(part, lows):
                mixed = nn(qkv[value_head(g), here], low).astype(BF16)
                for i in range(GROUP):
                    att[head(GROUP * g + i), here] = mixed[:, lanes(i)]
        if p == 0:
            weight(1)
        mixed = tn(wo[...], att[:, at])
        for b in range(buckets):
            middle[p, :, lanes(b)] = x_of(p, b) + mixed[:, lanes(b)]
        norm_forward(p, middle_of, 1, norm_two)
        if p == 0:
            weight(2)
            weight(3)
        for c in range(0, FF, CHUNK):
            rows = slice(c, c + CHUNK)
            gate = tn(wg[:, rows], norm_two[:, at])
            up = tn(wu[:, rows], norm_two[:, at])
            s = 1.0 / (1.0 + jnp.exp(-gate))
            silu = gate * s
            hidden[rows, at] = (silu * up).astype(BF16)
            d_up[rows, at] = silu.astype(BF16)
            d_gate[rows, at] = (up * (s + silu * (1.0 - s))).astype(BF16)
        if p == 0:
            weight(4)
        result = middle[p] + nn(wd[...], hidden[:, at])
        if p == 0:
            x_two[...] = result
        else:
            inputs[5].wait()
            for b in range(buckets):
                out_ref[b] = (result[:, lanes(b)] * alive[b]).astype(BF16)
                grad = cot_ref[b].astype(F32) * alive[b]
                dx_ref[b] = grad
                d_down[:, lanes(buckets + b)] = grad.astype(BF16)

    def put(first, block):
        low = block.astype(BF16)
        for h in range(2):
            for j in range(2):
                packed[h, first + j] = low[TILE_ROWS * h : TILE_ROWS * (h + 1), 128 * j : 128 * (j + 1)]

    def grad_down(h):
        per = FF // 2 // CHUNK
        for c in range(per):
            rows = pl.ds(pl.multiple_of(h * (FF // 2) + c * CHUNK, CHUNK), CHUNK)
            low = nt(d_down[...], hidden[rows, :]).astype(BF16)
            for i in range(2):
                for j in range(2):
                    packed[h, 6 * i + 2 * c + j] = low[TILE_ROWS * i : TILE_ROWS * (i + 1), 128 * j : 128 * (j + 1)]

    def grad_ffn(wave, d, part):
        for c in range(3 * part, 3 * part + 3):
            put(wave * TILES + 2 * c, nt(norm_two[...], d[c * CHUNK : (c + 1) * CHUNK, :]))

    def backward(p):
        at = slice(p * total, (p + 1) * total)
        if p == 0:
            grad_down(1 - core)
            red.after("down_a")
            grad_down(core)
            red.after("down_b")
        for c in range(0, FF, CHUNK):
            rows = slice(c, c + CHUNK)
            d_hidden = tn(wd[:, rows], d_down[:, at])
            d_up[rows, at] = (d_hidden * d_up[rows, at].astype(F32)).astype(BF16)
            d_gate[rows, at] = (d_hidden * d_gate[rows, at].astype(F32)).astype(BF16)
        if p == 0:
            red.after("gated")
            for wave, d, name in ((1, d_gate, "gate"), (2, d_up, "up")):
                grad_ffn(wave, d, 0)
                red.after(name + "_a")
                grad_ffn(wave, d, 1)
                red.after(name + "_b")
        dn[...] = nn(wg[...], d_gate[:, at]) + nn(wu[...], d_up[:, at])
        if p == 0:
            red.after("ffn")
        norm_backward(p, middle_of, 1, d_branch.at[:, at])
        if p == 0:
            red.after("norm_two")
        d_att[...] = nn(wo[...], d_branch[:, at]).astype(BF16)
        if p == 0:
            red.after("branch")
        todo = [(b, g) for b in range(buckets) for g in range(KV_HEADS)]
        for first in range(0, len(todo), ATTEND):
            part = todo[first : first + ATTEND]
            d_probs = [
                tn(qkv[value_head(g), lanes(p * buckets + b)], three(d_att, g, lanes(b))) for b, g in part
            ]
            d_scores = []
            for (b, g), d in zip(part, d_probs):
                pr = probs[p * buckets + b, g].astype(F32)
                d_scores.append((pr * (d - jnp.sum(d * pr, axis=0, keepdims=True))).astype(BF16))
            for (b, g), ds in zip(part, d_scores):
                here = lanes(p * buckets + b)
                d_query = nn(qkv[key_head(g), here], ds)
                for i in range(GROUP):
                    d_qkv[head(GROUP * g + i), here] = rope(d_query[:, lanes(i)], b, -1).astype(BF16)
                d_qkv[key_head(g), here] = rope(nt(three(qkv, g, here), ds), b, -1).astype(BF16)
                d_qkv[value_head(g), here] = nt(
                    three(d_att, g, lanes(b)), probs[p * buckets + b, g]
                ).astype(BF16)
            if p == 0:
                red.after("scores_a" if first == 0 else "scores_b")

    def backward_end(p):
        dn[...] = nn(wqkv[...], d_qkv[:, p * total : (p + 1) * total])
        if p == 0:
            red.after("qkv")
        norm_backward(p, x_of, 0, d_down.at[:, :total] if p == 1 else None)

    forward(0)
    forward(1)
    results = [pltpu.make_async_copy(out_ref, out_hbm, out_sem.at[0])]
    results[0].start()
    backward(1)
    backward_end(1)
    backward(0)

    column = lax.broadcasted_iota(jnp.int32, (1, CHUNK), 1)
    for c in range(3):
        block = nt(norm_one[...], d_qkv[c * CHUNK : (c + 1) * CHUNK, :])
        put(3 * TILES + 2 * c, block * jnp.where(column + c * CHUNK < D, scale, 1.0))
    block = nt(norm_one[...], d_qkv[3 * CHUNK :, :])
    rest = nt(att[...], d_branch[2 * CHUNK :, :])
    put(3 * TILES + 6, jnp.concatenate([block[:, : D + 2 * KVW - 3 * CHUNK], rest], axis=1))
    for c in range(2):
        put(3 * TILES + 8 + 2 * c, nt(att[...], d_branch[c * CHUNK : (c + 1) * CHUNK, :]))
    red.after("rest")
    backward_end(0)
    results.append(pltpu.make_async_copy(dx_ref, dx_hbm, out_sem.at[1]))
    results[1].start()
    for i in range(2):
        gain_buf[0, 0, i : i + 1, :D] = jnp.sum(gain_sum[i].T, axis=0, keepdims=True)
    red.gain_step()
    red.after("norm_one")
    red.after("end")
    while len(red.whole_gains) <= bits:
        red.gain_step()
    sums = gain_buf[0, bits + 1]
    gain_out_ref[...] = jnp.where(core == 0, sums, pltpu.roll(sums, 640 - TILE_ROWS, 1))
    for copy in red.started:
        copy.wait_send()
    for copy in results + red.leaving:
        copy.wait()


def run_layer(bits, lengths, tokens, cotangent, weights, gains):
    buckets = tokens.shape[0]
    total = buckets * BUCKET
    slots = WAVES * STREAMS
    half = (TILE_ROWS // 2, 128)
    steps = bits + 3
    vmem = pl.BlockSpec(memory_space=pltpu.VMEM)
    hbm = pl.BlockSpec(memory_space=pl.ANY)
    dma = pltpu.SemaphoreType.DMA
    grads = (WAVES * TILES, TILE_ROWS, 128)
    table = jnp.asarray(rope_table())
    scratch = [
        (tokens.shape, BF16), (tokens.shape, BF16), *((w.shape, BF16) for w in weights[:3]), (table.shape, BF16),
        (tokens.shape, BF16), (tokens.shape, F32), (grads, BF16),
        ((D, QKV), BF16), ((D, D), BF16), ((D, FF), BF16), ((D, FF), BF16), ((D, FF), BF16),
        ((8, 640), F32), ((8, 640), F32), ((2, D, BUCKET), F32), ((2, D, BUCKET), F32),
        ((HD, total), F32), ((buckets, BUCKET, BUCKET), F32),
        ((D, 2 * total), BF16), ((D, 2 * total), BF16), ((D, 2 * total), BF16),
        ((D, 2 * total), BF16), ((D, 2 * total), BF16),
        ((D + 2 * KVW, 2 * total), BF16),
        ((2 * buckets, KV_HEADS, BUCKET, GROUP * BUCKET), BF16),
        ((D, total), F32), ((2, D, total), F32),
        ((FF, 2 * total), BF16), ((FF, 2 * total), BF16), ((FF, 2 * total), BF16),
        ((D, total), F32), ((D, total), BF16), ((QKV, 2 * total), BF16),
        ((2, *grads), BF16), ((slots, 2, TILE_ROWS, 128), BF16), ((slots, TILE_ROWS, 128), BF16),
        ((slots, *half), BF16), ((slots, 2, bits - 3, *half), BF16), ((2, bits + 2, 8, 640), F32),
    ]
    return pl.pallas_call(
        functools.partial(layer_kernel, bits, buckets),
        out_shape=(
            jax.ShapeDtypeStruct((buckets, D, BUCKET), BF16),
            jax.ShapeDtypeStruct((buckets, D, BUCKET), F32),
            jax.ShapeDtypeStruct(grads, BF16),
            jax.ShapeDtypeStruct((8, 640), F32),
        ),
        in_specs=[pl.BlockSpec(memory_space=pltpu.SMEM)] + [hbm] * 9 + [vmem] * 2 + [hbm],
        out_specs=(hbm,) * 3 + (vmem,),
        scratch_shapes=[pltpu.VMEM(shape, dtype) for shape, dtype in scratch]
        + [
            dma((6,)), dma((6,)), dma((4,)), dma((WAVES,)), dma((WAVES,)), dma((slots, steps)),
            dma((slots, steps)), dma((bits + 1,)), dma((bits + 1,)), dma((slots,)), dma((6,)), dma((2,)),
        ],
        compiler_params=pltpu.CompilerParams(
            collective_id=0, has_side_effects=True, vmem_limit_bytes=63 << 20
        ),
    )(lengths, tokens, cotangent, *weights, *gains, table)


def unpack_kernel(
    res_hbm, out_in, dx_in, gain_in,
    out_ref, dx_ref, gq, gk, gv, go, gg, gu, gd, ga, gf,
    res_ref, out_block, dx_block, query, key, value, branch, gate, up, down, in_sem, out_sem,
):
    arrivals = [
        pltpu.make_async_copy(res_hbm.at[pl.ds(w * TILES, TILES)], res_ref.at[pl.ds(w * TILES, TILES)], in_sem.at[w])
        for w in range(WAVES)
    ]
    arrivals.append(pltpu.make_async_copy(dx_in, dx_block, in_sem.at[WAVES]))
    arrivals.append(pltpu.make_async_copy(out_in, out_block, in_sem.at[WAVES + 1]))
    for copy in arrivals:
        copy.start()
    copies = []
    ga[...] = gain_in[0, :TILE_ROWS]
    gf[...] = gain_in[1, :TILE_ROWS]

    def tile(t):
        return res_ref[t].astype(F32)

    def leave(src, dst):
        copy = pltpu.make_async_copy(src, dst, out_sem.at[len(copies)])
        copy.start()
        copies.append(copy)

    arrivals[0].wait()
    for j in range(6):
        for h in range(2):
            down[TILE_ROWS * h : TILE_ROWS * (h + 1), 128 * j : 128 * (j + 1)] = tile(6 * h + j)
    leave(down, gd)
    for w, block, dst in ((1, gate, gg), (2, up, gu)):
        arrivals[w].wait()
        for j in range(TILES):
            block[:, 128 * j : 128 * (j + 1)] = tile(w * TILES + j)
        leave(block, dst)
    arrivals[3].wait()
    first = 3 * TILES
    for j in range(4):
        query[:, 128 * j : 128 * (j + 1)] = tile(first + j)
        branch[:, 128 * j : 128 * (j + 1)] = tile(first + 8 + j)
    shared, last = tile(first + 4), tile(first + 7)
    query[:, 512:] = shared[:, :64]
    leave(query, gq)
    branch[:, 512:] = last[:, 64:]
    leave(branch, go)
    key[...] = jnp.concatenate([shared[:, 64:], tile(first + 5)], axis=1)
    leave(key, gk)
    value[...] = jnp.concatenate([tile(first + 6), last[:, :64]], axis=1)
    leave(value, gv)
    arrivals[WAVES].wait()
    leave(dx_block, dx_ref)
    arrivals[WAVES + 1].wait()
    leave(out_block, out_ref)
    for copy in copies:
        copy.wait()


def unpack(res, output, input_grad, gain_sum):
    shapes = [
        (TILE_ROWS, D), (TILE_ROWS, KVW), (TILE_ROWS, KVW), (TILE_ROWS, D), (TILE_ROWS, FF), (TILE_ROWS, FF),
        (D, FF // 2),
    ]
    vmem = pl.BlockSpec(memory_space=pltpu.VMEM)
    hbm = pl.BlockSpec(memory_space=pl.ANY)
    dma = pltpu.SemaphoreType.DMA
    return pl.pallas_call(
        unpack_kernel,
        out_shape=(
            jax.ShapeDtypeStruct(output.shape, output.dtype),
            jax.ShapeDtypeStruct(input_grad.shape, input_grad.dtype),
            *(jax.ShapeDtypeStruct(shape, F32) for shape in shapes + [(TILE_ROWS,)] * 2),
        ),
        in_specs=[hbm] * 3 + [vmem],
        out_specs=(hbm,) * 9 + (vmem,) * 2,
        scratch_shapes=[pltpu.VMEM(a.shape, a.dtype) for a in (res, output, input_grad)]
        + [pltpu.VMEM(shape, F32) for shape in shapes]
        + [dma((WAVES + 2,)), dma((len(shapes) + 2,))],
        compiler_params=pltpu.CompilerParams(vmem_limit_bytes=63 << 20),
    )(res, output, input_grad, gain_sum)


def on_device(
    bits, tokens, cotangent, lengths, w_query, w_key, w_value, w_out, w_gate, w_up, w_down, gain_attn, gain_ffn,
):
    output, input_grad, res, gain_sum = run_layer(
        bits,
        lengths[:, 0],
        tokens[:, 0].transpose(0, 2, 1),
        cotangent[:, 0].transpose(0, 2, 1),
        (w_query, w_key, w_value, w_out, w_gate, w_up, w_down.T),
        (gain_attn, gain_ffn),
    )
    output, input_grad, gq, gk, gv, go, gg, gu, gd, ga, gf = unpack(res, output, input_grad, gain_sum)
    return (
        output.transpose(0, 2, 1)[:, None], input_grad.transpose(0, 2, 1)[:, None],
        gq, gk, gv, go, gg, gu, gd.T, ga, gf,
    )


def solution(mesh):
    rows = P(None, ("dp", "fsdp"), None, None)
    weight = P("fsdp", None)
    in_specs = (rows, rows, P(None, ("dp", "fsdp"), None)) + (weight,) * 7 + (P("fsdp"),) * 2
    out_specs = (rows, rows) + (weight,) * 7 + (P("fsdp"),) * 2
    bits = mesh.shape["dp"].bit_length() - 1
    return jax.shard_map(
        functools.partial(on_device, bits),
        mesh=mesh,
        in_specs=in_specs,
        out_specs=out_specs,
        check_vma=False,
    )
```
